256 devices in a mesh: row: 8 (over y_hi, x), col: 32 (over z, y_lo, core).
Axes of the slice: x: 4, y: 4 (y_hi: 2, y_lo: 2; y = y_hi * 2 + y_lo), z: 8, core: 2. Of those that a mesh axis runs over, the one named last changes fastest.
Arguments:
- pair_field: float32 [512, 512, 128], P('row', 'col'), may hold values from -6 to 6
- token_mask: int32 [512], replicated, may hold values 0 or 1
- norm_in_gain: float32 [2, 128], replicated, may hold values from 0.1 to 1.9
- norm_in_shift: float32 [2, 128], replicated, may hold values from -3 to 3
- proj_in: bfloat16 [2, 128, 256], replicated, may hold values from -0.5 to 0.5
- gate_in: bfloat16 [2, 128, 256], replicated, may hold values from -0.5 to 0.5
- norm_out_gain: float32 [2, 128], replicated, may hold values from 0.1 to 1.9
- norm_out_shift: float32 [2, 128], replicated, may hold values from -3 to 3
- gate_out: bfloat16 [2, 128, 128], replicated, may hold values from -0.5 to 0.5
- proj_out: bfloat16 [2, 128, 128], replicated, may hold values from -0.5 to 0.5
Outputs:
- updated: float32 [512, 512, 128], P('row', 'col')
The draws below stay inside these ranges and needn't reach their ends.
All inputs are finite; a program needn't handle non-finite values.
Results may differ from the reference program's by a relative error of at most 0.007.
Values may be sent and summed in bfloat16 or wider, within the bound.
No kernel may reach another device: no remote copies, remote signals or barrier semaphores. Data moves between devices by JAX's collectives and lax.ppermute only.
A program may use at most 128 MiB of HBM per device.

```python
import jax
import jax.numpy as jnp
from jax import lax

PAIR_DIM = 128
HIDDEN_SIZE = 128
TOKENS = 512


def place_ends(drawn, own_key, smallest, top_value):
    longest = drawn.shape.index(max(drawn.shape))
    spots = []
    for shift in (0, 1):
        where = [jax.random.randint(jax.random.fold_in(own_key, axis), (), 0, length) for axis, length in enumerate(drawn.shape)]
        where[longest] = (where[longest] + shift) % drawn.shape[longest]
        spots.append(tuple(where))
    return drawn.at[spots[0]].set(smallest).at[spots[1]].set(top_value)


def level_of(rng, extent, shards, low, top_value):
    loudness, own = 1.0, jax.random.fold_in(rng, 6)
    for dim, blocks in shards:
        steps = jnp.exp(jax.random.uniform(jax.random.fold_in(own, dim), (blocks,), jnp.float32, low / len(shards), top_value / len(shards)))
        loudness = loudness * jnp.repeat(steps, extent[dim] // blocks).reshape([-1 if axis == dim else 1 for axis in range(len(extent))])
    return loudness


def gaussian(stream_key, extent, width, limit, cuts=(), dtype=jnp.bfloat16):
    factor_of = level_of(stream_key, extent, cuts, -0.22, 0.18) if cuts else 1.0
    array = jax.random.normal(stream_key, extent, jnp.float32) * width * factor_of
    return jnp.minimum(jnp.maximum(array, -limit), limit).astype(dtype)


def setup_inputs(seed: int = 0) -> dict:
    keys = jax.random.split(jax.random.key(seed), 11)
    pair_field = gaussian(keys[0], (TOKENS, TOKENS, PAIR_DIM), 1.0, 6.0, ((0, 8), (1, 32)), jnp.float32)
    token_mask = place_ends((jax.random.randint(keys[1], (TOKENS,), 0, 8) < 7).astype(jnp.int32), jax.random.fold_in(keys[1], 1), 0, 1)
    norm_in_gain = jnp.clip(1.0 + 0.18 * jax.random.normal(keys[2], (2, PAIR_DIM), jnp.float32), 0.1, 1.9)
    norm_in_shift = gaussian(keys[3], (2, PAIR_DIM), 0.5, 3.0, (), jnp.float32)
    proj_in = gaussian(keys[4], (2, PAIR_DIM, 2 * HIDDEN_SIZE), PAIR_DIM ** -0.5, 0.5)
    gate_in = gaussian(keys[5], (2, PAIR_DIM, 2 * HIDDEN_SIZE), PAIR_DIM ** -0.5, 0.5)
    norm_out_gain = jnp.clip(1.0 + 0.18 * jax.random.normal(keys[6], (2, HIDDEN_SIZE), jnp.float32), 0.1, 1.9)
    norm_out_shift = gaussian(keys[7], (2, HIDDEN_SIZE), 0.5, 3.0, (), jnp.float32)
    gate_out = gaussian(keys[8], (2, PAIR_DIM, PAIR_DIM), PAIR_DIM ** -0.5, 0.5)
    proj_out = gaussian(keys[9], (2, HIDDEN_SIZE, PAIR_DIM), HIDDEN_SIZE ** -0.5, 0.5)
    return dict(pair_field=pair_field, token_mask=token_mask, norm_in_gain=norm_in_gain, norm_in_shift=norm_in_shift, proj_in=proj_in, gate_in=gate_in, norm_out_gain=norm_out_gain, norm_out_shift=norm_out_shift, gate_out=gate_out, proj_out=proj_out)


epsilon = 1e-05

def layer_norm(values, scale_vec, offset_vec):
    average = lax.optimization_barrier(jnp.mean(values, axis=-1, keepdims=True))
    centred = values - average
    spread = lax.optimization_barrier(jnp.mean(centred * centred, axis=-1, keepdims=True))
    return centred * lax.rsqrt(spread + epsilon) * scale_vec + offset_vec

def triangle_update(pair_now, pair_weight, layer, incoming, norm_in_gain, norm_in_shift, proj_in, gate_in, norm_out_gain, norm_out_shift, gate_out, proj_out):
    normed = layer_norm(pair_now, norm_in_gain[layer], norm_in_shift[layer]).astype(jnp.bfloat16)
    projected = jnp.dot(normed, proj_in[layer], preferred_element_type=jnp.float32)
    gating = jnp.dot(normed, gate_in[layer], preferred_element_type=jnp.float32)
    halves = (jax.nn.sigmoid(gating) * projected * pair_weight[:, :, None]).astype(jnp.bfloat16)
    hidden = halves.shape[-1] // 2
    left_half = halves[..., :hidden].astype(jnp.float32)
    right_half = halves[..., hidden:].astype(jnp.float32)
    if incoming:
        combined = jnp.einsum('kic,kjc->ijc', left_half, right_half, precision=lax.Precision.HIGHEST)
    else:
        combined = jnp.einsum('ikc,jkc->ijc', left_half, right_half, precision=lax.Precision.HIGHEST)
    mixed = layer_norm(combined, norm_out_gain[layer], norm_out_shift[layer]).astype(jnp.bfloat16)
    out_gating = jax.nn.sigmoid(jnp.dot(normed, gate_out[layer], preferred_element_type=jnp.float32))
    return pair_now + out_gating * jnp.dot(mixed, proj_out[layer], preferred_element_type=jnp.float32)

def reference(pair_field, token_mask, norm_in_gain, norm_in_shift, proj_in, gate_in, norm_out_gain, norm_out_shift, gate_out, proj_out):
    valid = token_mask.astype(jnp.float32)
    pair_weight = valid[:, None] * valid[None, :]
    params = (norm_in_gain, norm_in_shift, proj_in, gate_in, norm_out_gain, norm_out_shift, gate_out, proj_out)
    first_pass = triangle_update(pair_field, pair_weight, 0, False, *params)
    return triangle_update(first_pass, pair_weight, 1, True, *params)
```

```python
import functools

import jax
import jax.numpy as jnp
import numpy as np
from jax import lax
from jax.experimental import pallas as pl
from jax.experimental.pallas import tpu as pltpu
from jax.sharding import Mesh
from jax.sharding import PartitionSpec as P

EPSILON = 1e-05
ROWS, LANES, HALF = 8, 128, 64
BF, F32 = jnp.bfloat16, jnp.float32
VMEM_LIMIT = 40 * 1024 * 1024


def sigmoid(x):
    return 0.5 * jnp.tanh(0.5 * x) + 0.5


def layer_norm(values, gain, shift, axis):
    average = jnp.mean(values, axis=axis, keepdims=True)
    centred = values - average
    spread = jnp.mean(centred * centred, axis=axis, keepdims=True)
    return centred * lax.rsqrt(spread + EPSILON) * gain + shift


def low_lanes(shape):
    return lax.broadcasted_iota(jnp.int32, shape, len(shape) - 1) < HALF


def swap_halves(first, second):
    low, axis = low_lanes(first.shape), first.ndim - 1
    return (
        jnp.where(low, first, pltpu.roll(second, HALF, axis)),
        jnp.where(low, pltpu.roll(first, HALF, axis), second),
    )


def project(chunk, s, weight, gain, shift, weights, staged, normed_ref):
    normed = layer_norm(chunk, gain, shift, -1).astype(BF)
    normed_ref[s] = normed
    both = lax.dot_general(weights, normed, (((1,), (1,)), ((), ())), preferred_element_type=F32)
    halves = sigmoid(both[2 * LANES :]) * both[: 2 * LANES] * weight
    staged[pl.ds(s, LANES, stride=2 * ROWS), :] = halves[:LANES]
    staged[pl.ds(ROWS + s, LANES, stride=2 * ROWS), :] = halves[LANES:]


def pair_weights(mask_vec, mask_smem):
    row, zy, core = lax.axis_index("row"), lax.axis_index("zy"), lax.axis_index("core")
    low = low_lanes((1, LANES))
    tokens = mask_vec[pl.ds(row // 2, 1), :].astype(F32)
    turned = pltpu.roll(tokens, HALF, 1)
    own = jnp.where(low == (row % 2 == 0), tokens, turned)
    begin = (zy * 2 + core) * (2 * ROWS)

    def weight(s):
        first = mask_smem[begin + s].astype(F32)
        second = mask_smem[begin + ROWS + s].astype(F32)
        return own * jnp.where(low, first, second)

    return weight


def joined_weights(proj_in, gate_in):
    return jnp.concatenate([proj_in[0].T, gate_in[0].T], axis=0)


def residual(prior, normed, gate_out, proj_out, combined, gain, shift):
    mixed = layer_norm(combined, gain, shift, 0).astype(BF)
    update = lax.dot_general(mixed, proj_out, (((0,), (0,)), ((), ())), preferred_element_type=F32)
    gating = jnp.dot(normed, gate_out, preferred_element_type=F32)
    return prior + sigmoid(gating) * update


def column(row_vec):
    return jnp.broadcast_to(row_vec, (LANES, LANES)).T


def tokens_of(pair_ref, s):
    return jnp.concatenate(
        [pair_ref[pl.ds(b * ROWS + s, HALF, stride=2 * ROWS), :] for b in range(2)], axis=0
    )


def first_kernel(pair_ref, mask_vec, mask_smem, gain, shift, proj_in, gate_in, send_ref, normed_ref, staged):
    weights = joined_weights(proj_in, gate_in)
    weight = pair_weights(mask_vec, mask_smem)
    for s in range(ROWS):
        project(tokens_of(pair_ref, s), s, weight(s), gain[0:1], shift[0:1], weights, staged, normed_ref)
    send_ref[...] = staged[...].astype(BF).reshape(send_ref.shape)


def second_kernel(
    back_ref, pair_ref, old_normed, mask_vec, mask_smem, gain, shift, proj_in, gate_in,
    out_gain, out_shift, gate_out, proj_out, send_ref, normed_ref, pass_ref, staged, wide,
):
    weights = joined_weights(proj_in, gate_in)
    weight = pair_weights(mask_vec, mask_smem)
    gain_col, shift_col = column(out_gain[0:1]), column(out_shift[0:1])
    wide[...] = back_ref[...].astype(F32).reshape(wide.shape)
    for s in range(ROWS):
        combined = wide[pl.ds(s, LANES, stride=ROWS), :]
        first_pass = residual(
            tokens_of(pair_ref, s), old_normed[s], gate_out[0], proj_out[0], combined, gain_col, shift_col
        )
        pass_ref[s] = first_pass
        project(first_pass, s, weight(s), gain[1:2], shift[1:2], weights, staged, normed_ref)
    send_ref[...] = staged[...].astype(BF).reshape(send_ref.shape)


def third_kernel(
    back_ref, pass_ref, old_normed, out_gain, out_shift, gate_out, proj_out, out_ref, wide
):
    gain_col, shift_col = column(out_gain[1:2]), column(out_shift[1:2])
    wide[...] = back_ref[...].astype(F32).reshape(wide.shape)
    for s in range(ROWS):
        combined = wide[pl.ds(s, LANES, stride=ROWS), :]
        updated = residual(
            pass_ref[s], old_normed[s], gate_out[0], proj_out[0], combined, gain_col, shift_col
        )
        for b in range(2):
            out_ref[pl.ds(b * ROWS + s, HALF, stride=2 * ROWS), :] = updated[b * HALF : (b + 1) * HALF]


def triangle_kernel(incoming, own_ref, other_ref, out_ref, left, right, *rest):
    core = lax.axis_index("core")
    groups = own_ref.shape[0] // ROWS
    for ref, place, mine in ((own_ref, core, True), (other_ref, 1 - core, False)):
        for m in range(ROWS // 2):
            lanes = pl.ds(m * LANES, LANES)
            first = ref[pl.ds(2 * m * groups, groups)].astype(F32)
            second = ref[pl.ds((2 * m + 1) * groups, groups)].astype(F32)
            low, high = swap_halves(first[:, :ROWS], second[:, :ROWS])
            left[:, place, :, lanes] = jnp.concatenate([low, high], axis=1).astype(BF)
            if mine or not incoming:
                low, high = swap_halves(first[:, ROWS:], second[:, ROWS:])
                tile = jnp.concatenate([low, high], axis=1).astype(BF)
                if incoming:
                    right[:, :, lanes] = tile
                else:
                    right[:, place, :, lanes] = tile
    tokens = groups * 4 * ROWS
    lefts = left[...].reshape(tokens, tokens)
    if incoming:
        rights = right[...].reshape(tokens // 2, tokens)
        product = lax.dot_general(rights, lefts, (((1,), (1,)), ((), ())), preferred_element_type=F32)
        product = product.reshape(groups, 2 * ROWS, tokens)
    else:
        rights = right[...].reshape(tokens, tokens)
        (total,) = rest
        total[...] = lax.dot_general(
            rights, lefts, (((0,), (0,)), ((), ())), preferred_element_type=F32
        ).reshape(total.shape)
        product = total[:, core]
    for m in range(ROWS // 2):
        part = product[:, :, m * LANES : (m + 1) * LANES]
        even, odd = swap_halves(part[:, :ROWS], part[:, ROWS:])
        out_ref[pl.ds(2 * m * groups, groups)] = even.astype(BF)
        out_ref[pl.ds((2 * m + 1) * groups, groups)] = odd.astype(BF)


def whole(shape):
    return pl.BlockSpec(shape, lambda i: (0,) * len(shape))


def layer_of(array, layer):
    return pl.BlockSpec((1, *array.shape[1:]), lambda i: (layer, 0, 0))


SMEM = pl.BlockSpec(memory_space=pltpu.SMEM)


def call(body, in_specs, out_shapes, scratch, name):
    return pl.pallas_call(
        body,
        grid=(1,),
        in_specs=in_specs,
        out_specs=[whole(o.shape) for o in out_shapes],
        out_shape=out_shapes,
        scratch_shapes=scratch,
        compiler_params=pltpu.CompilerParams(vmem_limit_bytes=VMEM_LIMIT),
        name=name,
    )


def on_device(chips, pair_field, token_mask, gain, shift, proj_in, gate_in, out_gain, out_shift, gate_out, proj_out):
    tokens = pair_field.shape[0] * pair_field.shape[1]
    channels = pair_field.shape[2]
    pairs = pair_field.reshape(tokens, channels)
    mask_vec = token_mask.reshape(-1, LANES)
    shape = jax.ShapeDtypeStruct
    send = shape((chips, 2 * ROWS, LANES), BF)
    back = shape((chips, ROWS, LANES), BF)
    kept = shape((ROWS, LANES, channels), BF)
    staged = pltpu.VMEM((channels * 2 * ROWS, LANES), F32)
    wide = pltpu.VMEM((channels * ROWS, LANES), F32)
    vectors = [whole(gain.shape)] * 2

    def exchange(x):
        return lax.all_to_all(x, ("row", "zy"), 0, 0, tiled=True)

    def triangle(sent, incoming):
        mine = exchange(sent)
        other = lax.ppermute(mine, "core", [(0, 1), (1, 0)])
        n = token_mask.shape[0]
        both = (n // 32, 2, 16, n)
        scratch = [pltpu.VMEM(both, BF)]
        if incoming:
            scratch += [pltpu.VMEM((n // 32, 16, n), BF)]
        else:
            scratch += [pltpu.VMEM(both, BF), pltpu.VMEM(both, F32)]
        (result,) = call(
            functools.partial(triangle_kernel, incoming),
            [whole(send.shape)] * 2,
            [back],
            scratch,
            "incoming" if incoming else "outgoing",
        )(mine, other)
        return exchange(result)

    sent, normed = call(
        first_kernel,
        [whole(pairs.shape), whole(mask_vec.shape), SMEM, *vectors, layer_of(proj_in, 0), layer_of(gate_in, 0)],
        [send, kept],
        [staged],
        "project_first",
    )(pairs, mask_vec, token_mask, gain, shift, proj_in, gate_in)
    combined = triangle(sent, False)
    sent, normed, first_pass = call(
        second_kernel,
        [
            whole(back.shape), whole(pairs.shape), whole(kept.shape), whole(mask_vec.shape), SMEM, *vectors,
            layer_of(proj_in, 1), layer_of(gate_in, 1), *vectors, layer_of(gate_out, 0), layer_of(proj_out, 0),
        ],
        [send, kept, shape(kept.shape, F32)],
        [staged, wide],
        "finish_and_project",
    )(
        combined, pairs, normed, mask_vec, token_mask, gain, shift, proj_in, gate_in,
        out_gain, out_shift, gate_out, proj_out,
    )
    combined = triangle(sent, True)
    (updated,) = call(
        third_kernel,
        [
            whole(back.shape), whole(kept.shape), whole(kept.shape), *vectors,
            layer_of(gate_out, 1), layer_of(proj_out, 1),
        ],
        [shape(pairs.shape, F32)],
        [wide],
        "finish",
    )(combined, first_pass, normed, out_gain, out_shift, gate_out, proj_out)
    return updated.reshape(pair_field.shape)


def solution(mesh):
    rows, cols = mesh.devices.shape
    split = Mesh(np.asarray(mesh.devices).reshape(rows, cols // 2, 2), ("row", "zy", "core"))
    spec = P("row", ("zy", "core"), None)
    return jax.shard_map(
        functools.partial(on_device, rows * cols // 2),
        mesh=split,
        in_specs=(spec,) + (P(),) * 9,
        out_specs=spec,
        check_vma=False,
    )
```

```python
import functools

import jax
import jax.numpy as jnp
import numpy as np
from jax import lax
from jax.experimental import pallas as pl
from jax.experimental.pallas import tpu as pltpu
from jax.sharding import Mesh
from jax.sharding import PartitionSpec as P

EPSILON = 1e-05
ROWS, LANES, HALF = 8, 128, 64
BF, F32 = jnp.bfloat16, jnp.float32
VMEM_LIMIT = 40 * 1024 * 1024
ORDER = ("z", "y", "h", "x")


def sigmoid(x):
    return 0.5 * jnp.tanh(0.5 * x) + 0.5


def layer_norm(values, gain, shift, axis):
    average = jnp.mean(values, axis=axis, keepdims=True)
    centred = values - average
    spread = jnp.mean(centred * centred, axis=axis, keepdims=True)
    return centred * lax.rsqrt(spread + EPSILON) * gain + shift


def low_lanes(shape):
    return lax.broadcasted_iota(jnp.int32, shape, len(shape) - 1) < HALF


def swap_halves(first, second):
    low, axis = low_lanes(first.shape), first.ndim - 1
    return (
        jnp.where(low, first, pltpu.roll(second, HALF, axis)),
        jnp.where(low, pltpu.roll(first, HALF, axis), second),
    )


def project(chunk, s, weight, gain, shift, weights, staged, normed_ref):
    normed = layer_norm(chunk, gain, shift, -1).astype(BF)
    normed_ref[s] = normed
    both = lax.dot_general(weights, normed, (((1,), (1,)), ((), ())), preferred_element_type=F32)
    halves = sigmoid(both[2 * LANES :]) * both[: 2 * LANES] * weight
    staged[pl.ds(s, LANES, stride=2 * ROWS), :] = halves[:LANES]
    staged[pl.ds(ROWS + s, LANES, stride=2 * ROWS), :] = halves[LANES:]


def joined_weights(proj_in, gate_in):
    return jnp.concatenate([proj_in.T, gate_in.T], axis=0)


def residual(prior, gating, proj_out, combined, gain, shift):
    mixed = layer_norm(combined, gain, shift, 0).astype(BF)
    update = lax.dot_general(mixed, proj_out, (((0,), (0,)), ((), ())), preferred_element_type=F32)
    return prior + gating * update


def tokens_of(pair_ref, s):
    return jnp.concatenate(
        [pair_ref[pl.ds(b * ROWS + s, HALF, stride=2 * ROWS), :] for b in range(2)], axis=0
    )


def first_kernel(
    pair_hbm, mask_hbm, lanes_hbm, gain_hbm, shift_hbm, proj_hbm, gate_hbm,
    send_ref, normed_ref, weight_ref,
    pair_ref, mask_vec, mask_smem, gain, shift, proj_in, gate_in, staged, arrived,
):
    moves = [
        (proj_hbm.at[0], proj_in),
        (gate_hbm.at[0], gate_in),
        (pair_hbm, pair_ref),
        (mask_hbm, mask_smem),
        (lanes_hbm, mask_vec),
        (gain_hbm, gain),
        (shift_hbm, shift),
    ]
    copies = [
        pltpu.make_async_copy(src, dst, arrived.at[n]) for n, (src, dst) in enumerate(moves)
    ]
    for copy in copies:
        copy.start()
    for copy in copies[:2]:
        copy.wait()
    weights = joined_weights(proj_in[...], gate_in[...])
    for copy in copies[2:]:
        copy.wait()
    row, core = lax.axis_index(("h", "x")), lax.axis_index("core")
    chip = lax.axis_index("z") * 2 + lax.axis_index("y")
    low = low_lanes((1, LANES))
    tokens = mask_vec[pl.ds(row // 2, 1), :].astype(F32)
    own = jnp.where(low == (row % 2 == 0), tokens, pltpu.roll(tokens, HALF, 1))
    begin = (chip * 2 + core) * (2 * ROWS)
    for s in range(ROWS):
        first = mask_smem[begin + s].astype(F32)
        second = mask_smem[begin + ROWS + s].astype(F32)
        weight = own * jnp.where(low, first, second)
        weight_ref[pl.ds(s, 1), :] = weight
        project(tokens_of(pair_ref, s), s, weight, gain[0:1], shift[0:1], weights, staged, normed_ref)
    weight_ref[pl.ds(ROWS, 1), :] = gain[1:2]
    weight_ref[pl.ds(ROWS + 1, 1), :] = shift[1:2]
    send_ref[...] = staged[...].astype(BF).reshape(send_ref.shape)


def gates_kernel(normed_ref, gate_out, gates_ref):
    for s in range(ROWS):
        gates_ref[s] = sigmoid(jnp.dot(normed_ref[s], gate_out[0], preferred_element_type=F32))


def aside_kernel(
    pair_ref, normed_ref, gate_out, proj_in, gate_in, out_gain, out_shift,
    prior_ref, gates_ref, weights_ref, columns_ref,
):
    gates_kernel(normed_ref, gate_out, gates_ref)
    for s in range(ROWS):
        prior_ref[s] = tokens_of(pair_ref, s)
    weights_ref[...] = joined_weights(proj_in[0], gate_in[0])
    for layer in range(2):
        for n, ref in enumerate((out_gain, out_shift)):
            row_vec = ref[layer : layer + 1]
            columns_ref[layer, n] = jnp.broadcast_to(row_vec, (LANES, LANES)).T


def second_kernel(
    back_ref, prior_ref, gates_ref, weights_ref, columns_ref, weight_ref, proj_out,
    send_ref, normed_ref, pass_ref, staged, wide,
):
    wide[...] = back_ref[...].astype(F32).reshape(wide.shape)
    gain, shift = weight_ref[pl.ds(ROWS, 1), :], weight_ref[pl.ds(ROWS + 1, 1), :]
    for s in range(ROWS):
        combined = wide[pl.ds(s, LANES, stride=ROWS), :]
        first_pass = residual(
            prior_ref[s], gates_ref[s], proj_out[0], combined, columns_ref[0, 0], columns_ref[0, 1]
        )
        pass_ref[s] = first_pass
        weight = weight_ref[pl.ds(s, 1), :]
        project(first_pass, s, weight, gain, shift, weights_ref[...], staged, normed_ref)
    send_ref[...] = staged[...].astype(BF).reshape(send_ref.shape)


def third_kernel(back_ref, pass_ref, gates_ref, columns_ref, proj_out, out_ref, wide):
    wide[...] = back_ref[...].astype(F32).reshape(wide.shape)
    for s in range(ROWS):
        combined = wide[pl.ds(s, LANES, stride=ROWS), :]
        updated = residual(
            pass_ref[s], gates_ref[s], proj_out[0], combined, columns_ref[1, 0], columns_ref[1, 1]
        )
        for b in range(2):
            out_ref[pl.ds(b * ROWS + s, HALF, stride=2 * ROWS), :] = updated[b * HALF : (b + 1) * HALF]


def of_row(row, wide_x):
    at = {"h": row // wide_x, "x": row % wide_x}
    return tuple(at.get(axis, slice(None)) for axis in ORDER)


def columns_first(block):
    if ORDER.index("z") < ORDER.index("y"):
        return block
    return jnp.swapaxes(block, 0, 1)


def triangle_kernel(incoming, own_ref, other_ref, out_ref, left, right, *rest):
    core = lax.axis_index("core")
    wide_x = own_ref.shape[ORDER.index("x")]
    for ref, place, mine in ((own_ref, core, True), (other_ref, 1 - core, False)):
        for m in range(ROWS // 2):
            lanes = pl.ds(m * LANES, LANES)
            first = columns_first(ref[of_row(2 * m, wide_x)].astype(F32))
            second = columns_first(ref[of_row(2 * m + 1, wide_x)].astype(F32))
            low, high = swap_halves(first[:, :, :ROWS], second[:, :, :ROWS])
            left[:, :, place, :, lanes] = jnp.concatenate([low, high], axis=2).astype(BF)
            if mine or not incoming:
                low, high = swap_halves(first[:, :, ROWS:], second[:, :, ROWS:])
                tile = jnp.concatenate([low, high], axis=2).astype(BF)
                if incoming:
                    right[:, :, :, lanes] = tile
                else:
                    right[:, :, place, :, lanes] = tile
    tokens = left.shape[-1]
    lefts = left[...].reshape(tokens, tokens)
    if incoming:
        rights = right[...].reshape(tokens // 2, tokens)
        product = lax.dot_general(rights, lefts, (((1,), (1,)), ((), ())), preferred_element_type=F32)
        product = product.reshape(right.shape)
    else:
        rights = right[...].reshape(tokens, tokens)
        (total,) = rest
        total[...] = lax.dot_general(
            rights, lefts, (((0,), (0,)), ((), ())), preferred_element_type=F32
        ).reshape(total.shape)
        product = total[:, :, core]
    for m in range(ROWS // 2):
        part = product[..., m * LANES : (m + 1) * LANES]
        even, odd = swap_halves(part[:, :, :ROWS], part[:, :, ROWS:])
        out_ref[of_row(2 * m, wide_x)] = columns_first(even.astype(BF))
        out_ref[of_row(2 * m + 1, wide_x)] = columns_first(odd.astype(BF))


def whole(shape):
    return pl.BlockSpec(shape, lambda i: (0,) * len(shape))


def layer_of(array, layer):
    return pl.BlockSpec((1, *array.shape[1:]), lambda i: (layer, 0, 0))


HBM = pl.BlockSpec(memory_space=pltpu.HBM)


def call(body, in_specs, out_shapes, scratch, name, flops=None):
    cost = None
    if flops is not None:
        cost = pl.CostEstimate(flops=flops, bytes_accessed=4 * 2**20, transcendentals=2**17)
    return pl.pallas_call(
        body,
        grid=(1,),
        in_specs=in_specs,
        out_specs=[whole(o.shape) for o in out_shapes],
        out_shape=out_shapes,
        scratch_shapes=scratch,
        compiler_params=pltpu.CompilerParams(vmem_limit_bytes=VMEM_LIMIT),
        cost_estimate=cost,
        name=name,
    )


def on_device(chips, pair_field, token_mask, gain, shift, proj_in, gate_in, out_gain, out_shift, gate_out, proj_out):
    tokens = pair_field.shape[0] * pair_field.shape[1]
    channels = pair_field.shape[2]
    pairs = pair_field.reshape(tokens, channels)
    mask_vec = token_mask.reshape(-1, LANES)
    shape = jax.ShapeDtypeStruct
    send = shape((chips, 2 * ROWS, LANES), BF)
    back = shape((chips, ROWS, LANES), BF)
    kept = shape((ROWS, LANES, channels), BF)
    kept_wide = shape(kept.shape, F32)
    joined = shape((4 * channels, channels), BF)
    columns = shape((2, 2, channels, LANES), F32)
    weight = shape((2 * ROWS, LANES), F32)
    staged = pltpu.VMEM((channels * 2 * ROWS, LANES), F32)
    wide = pltpu.VMEM((channels * ROWS, LANES), F32)
    vectors = [whole(gain.shape)] * 2
    gate_flops = 2 * tokens * channels * channels

    def exchange(x):
        return lax.all_to_all(x, ORDER, 0, 0, tiled=True)

    by_chip = tuple(lax.axis_size(axis) for axis in ORDER)

    def triangle(sent, incoming, aside):
        mine = exchange(sent)
        mine, *aside[1:] = lax.optimization_barrier([mine, *aside[1:]])
        other = lax.ppermute(mine, "core", [(0, 1), (1, 0)])
        kept_aside = aside[0](*aside[1:])
        other, kept_aside = lax.optimization_barrier((other, kept_aside))
        n = token_mask.shape[0]
        both = (n // 64, 2, 2, 16, n)
        scratch = [pltpu.VMEM(both, BF)]
        if incoming:
            scratch += [pltpu.VMEM((n // 64, 2, 16, n), BF)]
        else:
            scratch += [pltpu.VMEM(both, BF), pltpu.VMEM(both, F32)]
        (result,) = call(
            functools.partial(triangle_kernel, incoming),
            [whole(by_chip + send.shape[1:])] * 2,
            [shape(by_chip + back.shape[1:], BF)],
            scratch,
            "incoming" if incoming else "outgoing",
        )(mine.reshape(by_chip + send.shape[1:]), other.reshape(by_chip + send.shape[1:]))
        return exchange(result.reshape(back.shape)), kept_aside

    sent, normed, weights = call(
        first_kernel,
        [HBM] * 7,
        [send, kept, weight],
        [
            pltpu.VMEM(pairs.shape, F32),
            pltpu.VMEM(mask_vec.shape, jnp.int32),
            pltpu.SMEM(token_mask.shape, jnp.int32),
            pltpu.VMEM(gain.shape, F32),
            pltpu.VMEM(shift.shape, F32),
            pltpu.VMEM(proj_in.shape[1:], BF),
            pltpu.VMEM(gate_in.shape[1:], BF),
            staged,
            pltpu.SemaphoreType.DMA((7,)),
        ],
        "project_first",
    )(*(
        pltpu.with_memory_space_constraint(x, pltpu.HBM)
        for x in (pairs, token_mask, mask_vec, gain, shift, proj_in, gate_in)
    ))
    aside = call(
        aside_kernel,
        [
            whole(pairs.shape), whole(kept.shape), layer_of(gate_out, 0),
            layer_of(proj_in, 1), layer_of(gate_in, 1), *vectors,
        ],
        [kept_wide, kept_wide, joined, columns],
        [],
        "aside",
        gate_flops,
    )
    combined, (prior, gates, second_weights, column_vectors) = triangle(
        sent, False, [aside, pairs, normed, gate_out, proj_in, gate_in, out_gain, out_shift]
    )
    sent, normed, first_pass = call(
        second_kernel,
        [
            whole(back.shape), whole(kept.shape), whole(kept.shape), whole(joined.shape),
            whole(columns.shape), whole(weight.shape), layer_of(proj_out, 0),
        ],
        [send, kept, kept_wide],
        [staged, wide],
        "finish_and_project",
    )(combined, prior, gates, second_weights, column_vectors, weights, proj_out)
    aside = call(
        gates_kernel,
        [whole(kept.shape), layer_of(gate_out, 1)],
        [kept_wide],
        [],
        "output_gates",
        gate_flops,
    )
    combined, (gates,) = triangle(sent, True, [aside, normed, gate_out])
    (updated,) = call(
        third_kernel,
        [whole(back.shape), whole(kept.shape), whole(kept.shape), whole(columns.shape), layer_of(proj_out, 1)],
        [shape(pairs.shape, F32)],
        [wide],
        "finish",
    )(combined, first_pass, gates, column_vectors, proj_out)
    return updated.reshape(pair_field.shape)


def solution(mesh):
    rows, cols = mesh.devices.shape
    devices = np.asarray(mesh.devices).reshape(2, rows // 2, cols // 4, 2, 2)
    spec = P(("h", "x"), ("z", "y", "core"), None)
    return jax.shard_map(
        functools.partial(on_device, rows * cols // 2),
        mesh=Mesh(devices, ("h", "x", "z", "y", "core")),
        in_specs=(spec,) + (P(),) * 9,
        out_specs=spec,
        check_vma=False,
    )
```

```python
import functools

import jax
import jax.numpy as jnp
import numpy as np
from jax import lax
from jax.experimental import pallas as pl
from jax.experimental.pallas import tpu as pltpu
from jax.sharding import Mesh
from jax.sharding import PartitionSpec as P

EPSILON = 1e-05
ROWS, LANES, HALF = 8, 128, 64
BF, F32 = jnp.bfloat16, jnp.float32
VMEM_LIMIT = 40 * 1024 * 1024
ORDER = ("z", "y", "h", "x")
Z_LIST = (0, 4, 1, 5, 2, 6, 3, 7)


def sigmoid(x):
    return 0.5 * jnp.tanh(0.5 * x) + 0.5


def layer_norm(values, gain, shift, axis):
    average = jnp.mean(values, axis=axis, keepdims=True)
    centred = values - average
    spread = jnp.mean(centred * centred, axis=axis, keepdims=True)
    return centred * lax.rsqrt(spread + EPSILON) * gain + shift


def low_lanes(shape):
    return lax.broadcasted_iota(jnp.int32, shape, len(shape) - 1) < HALF


def swap_halves(first, second):
    low, axis = low_lanes(first.shape), first.ndim - 1
    return (
        jnp.where(low, first, pltpu.roll(second, HALF, axis)),
        jnp.where(low, pltpu.roll(first, HALF, axis), second),
    )


def project(chunk, s, weight, gain, shift, weights, staged, normed_ref):
    normed = layer_norm(chunk, gain, shift, -1).astype(BF)
    normed_ref[s : s + 2] = normed.reshape(2, LANES, LANES)
    both = lax.dot_general(weights, normed, (((1,), (1,)), ((), ())), preferred_element_type=F32)
    halves = sigmoid(both[2 * LANES :]) * both[: 2 * LANES] * weight
    for n in range(2):
        part = halves[:, n * LANES : (n + 1) * LANES]
        staged[pl.ds(s + n, LANES, stride=2 * ROWS), :] = part[:LANES]
        staged[pl.ds(ROWS + s + n, LANES, stride=2 * ROWS), :] = part[LANES:]


def joined_weights(proj_in, gate_in):
    return jnp.concatenate([proj_in.T, gate_in.T], axis=0)


def pair_of(ref, s):
    return ref[s : s + 2].reshape(2 * LANES, LANES)


def residual(prior_ref, gates_ref, proj_out, wide, columns_ref, layer, s):
    parts = [wide[pl.ds(s + n, LANES, stride=ROWS), :] for n in range(2)]
    gain, shift = (jnp.concatenate([columns_ref[layer, n]] * 2, axis=1) for n in range(2))
    mixed = layer_norm(jnp.concatenate(parts, axis=1), gain, shift, 0).astype(BF)
    update = lax.dot_general(mixed, proj_out, (((0,), (0,)), ((), ())), preferred_element_type=F32)
    return pair_of(prior_ref, s) + pair_of(gates_ref, s) * update


def tokens_of(pair_ref, s):
    return jnp.concatenate(
        [pair_ref[pl.ds(b * ROWS + s, HALF, stride=2 * ROWS), :] for b in range(2)], axis=0
    )


def first_kernel(
    pair_hbm, mask_hbm, lanes_hbm, gain_hbm, shift_hbm, out_gain_hbm, out_shift_hbm, proj_hbm, gate_hbm,
    send_ref, normed_ref, weight_ref, vectors_ref,
    pair_ref, mask_vec, mask_smem, gain, shift, out_gain, out_shift, proj_in, gate_in, staged, arrived,
):
    moves = [
        (proj_hbm.at[0], proj_in),
        (gate_hbm.at[0], gate_in),
        (pair_hbm, pair_ref),
        (mask_hbm, mask_smem),
        (lanes_hbm, mask_vec),
        (gain_hbm, gain),
        (shift_hbm, shift),
        (out_gain_hbm, out_gain),
        (out_shift_hbm, out_shift),
    ]
    copies = [
        pltpu.make_async_copy(src, dst, arrived.at[n]) for n, (src, dst) in enumerate(moves)
    ]
    for copy in copies:
        copy.start()
    for copy in copies[:2]:
        copy.wait()
    weights = joined_weights(proj_in[...], gate_in[...])
    for copy in copies[2:]:
        copy.wait()
    row, core = lax.axis_index(("h", "x")), lax.axis_index("core")
    chip = lax.axis_index("z") * 2 + lax.axis_index("y")
    low = low_lanes((1, LANES))
    tokens = mask_vec[pl.ds(row // 2, 1), :].astype(F32)
    own = jnp.where(low == (row % 2 == 0), tokens, pltpu.roll(tokens, HALF, 1))
    begin = (chip * 2 + core) * (2 * ROWS)
    for s in range(0, ROWS, 2):
        both = []
        for n in range(2):
            first = mask_smem[begin + s + n].astype(F32)
            second = mask_smem[begin + ROWS + s + n].astype(F32)
            weight = own * jnp.where(low, first, second)
            weight_ref[pl.ds(s + n, 1), :] = weight
            both.append(weight)
        chunk = jnp.concatenate([tokens_of(pair_ref, s), tokens_of(pair_ref, s + 1)], axis=0)
        weight = jnp.concatenate(both, axis=1)
        project(chunk, s, weight, gain[0:1], shift[0:1], weights, staged, normed_ref)
    send_ref[...] = staged[...].astype(BF).reshape(send_ref.shape)
    for n, ref in enumerate((gain, shift, out_gain, out_shift)):
        vectors_ref[pl.ds(2 * n, 2), :] = ref[...]


def gates_of(normed_ref, gate_out, gates_ref):
    for s in range(0, ROWS, 2):
        gating = jnp.dot(pair_of(normed_ref, s), gate_out[0], preferred_element_type=F32)
        gates_ref[s : s + 2] = sigmoid(gating).reshape(2, LANES, LANES)


def second_kernel(
    back_ref, prior_ref, gates_ref, weights_ref, columns_ref, weight_ref, vectors_ref, proj_out,
    send_ref, normed_ref, pass_ref, staged, wide,
):
    wide[...] = back_ref[...].astype(F32).reshape(wide.shape)
    gain, shift = vectors_ref[pl.ds(1, 1), :], vectors_ref[pl.ds(3, 1), :]
    for s in range(0, ROWS, 2):
        first_pass = residual(prior_ref, gates_ref, proj_out[0], wide, columns_ref, 0, s)
        pass_ref[s : s + 2] = first_pass.reshape(2, LANES, LANES)
        weight = jnp.concatenate([weight_ref[pl.ds(s + n, 1), :] for n in range(2)], axis=1)
        project(first_pass, s, weight, gain, shift, weights_ref[...], staged, normed_ref)
    send_ref[...] = staged[...].astype(BF).reshape(send_ref.shape)


def third_kernel(back_ref, pass_ref, gates_ref, columns_ref, proj_out, out_ref, wide):
    wide[...] = back_ref[...].astype(F32).reshape(wide.shape)
    for s in range(0, ROWS, 2):
        updated = residual(pass_ref, gates_ref, proj_out[0], wide, columns_ref, 1, s)
        for n in range(4):
            place = n % 2 * ROWS + s + n // 2
            out_ref[pl.ds(place, HALF, stride=2 * ROWS), :] = updated[n * HALF : (n + 1) * HALF]


def of_row(row, wide_x):
    at = {"h": row // wide_x, "x": row % wide_x}
    return tuple(at.get(axis, slice(None)) for axis in ORDER)


def columns_first(block):
    if ORDER.index("z") > ORDER.index("y"):
        block = jnp.swapaxes(block, 0, 1)
    return jnp.stack([block[Z_LIST.index(z)] for z in range(len(Z_LIST))])


def as_listed(block):
    block = jnp.stack([block[z] for z in Z_LIST])
    return jnp.swapaxes(block, 0, 1) if ORDER.index("z") > ORDER.index("y") else block


def gather_rows(ref, half, store):
    wide_x = ref.shape[ORDER.index("x")]
    rows = slice(half * ROWS, (half + 1) * ROWS)
    for m in range(ROWS // 2):
        first = columns_first(ref[of_row(2 * m, wide_x)].astype(F32))
        second = columns_first(ref[of_row(2 * m + 1, wide_x)].astype(F32))
        low, high = swap_halves(first[:, :, rows], second[:, :, rows])
        store(pl.ds(m * LANES, LANES), jnp.concatenate([low, high], axis=2).astype(BF))


def scatter_rows(product, out_ref):
    wide_x = out_ref.shape[ORDER.index("x")]
    for m in range(ROWS // 2):
        part = product[..., m * LANES : (m + 1) * LANES]
        even, odd = swap_halves(part[:, :, :ROWS], part[:, :, ROWS:])
        out_ref[of_row(2 * m, wide_x)] = as_listed(even.astype(BF))
        out_ref[of_row(2 * m + 1, wide_x)] = as_listed(odd.astype(BF))


def keep_in(ref):
    def store(lanes, tile):
        ref[:, :, :, lanes] = tile

    return store


def outgoing_product(ref, left, right, total):
    gather_rows(ref, 0, keep_in(left))
    gather_rows(ref, 1, keep_in(right))
    tokens = left.shape[-1]
    lefts, rights = left[...].reshape(-1, tokens), right[...].reshape(-1, tokens)
    total[...] = lax.dot_general(
        rights, lefts, (((0,), (0,)), ((), ())), preferred_element_type=F32
    ).reshape(total.shape)
    return total[:, :, lax.axis_index("core")]


def outgoing_own_kernel(
    own_ref, pair_ref, normed_ref, gate_out, proj_in, gate_in, vectors_ref,
    partial_ref, prior_ref, gates_ref, weights_ref, columns_ref, left, right, total,
):
    partial_ref[...] = outgoing_product(own_ref, left, right, total)
    gates_of(normed_ref, gate_out, gates_ref)
    for s in range(ROWS):
        prior_ref[s] = tokens_of(pair_ref, s)
    weights_ref[...] = joined_weights(proj_in[0], gate_in[0])
    for layer in range(2):
        for n in range(2):
            row_vec = vectors_ref[pl.ds(4 + 2 * n + layer, 1), :]
            columns_ref[layer, n] = jnp.broadcast_to(row_vec, (LANES, LANES)).T


def outgoing_kernel(other_ref, partial_ref, out_ref, left, right, total):
    scatter_rows(partial_ref[...] + outgoing_product(other_ref, left, right, total), out_ref)


def incoming_own_kernel(own_ref, normed_ref, gate_out, left_ref, right_ref, gates_ref):
    gather_rows(own_ref, 0, keep_in(left_ref))
    gather_rows(own_ref, 1, keep_in(right_ref))
    gates_of(normed_ref, gate_out, gates_ref)


def incoming_kernel(other_ref, left_ref, right_ref, out_ref, left):
    core = lax.axis_index("core")
    left[:, :, core] = left_ref[...]

    def store(lanes, tile):
        left[:, :, 1 - core, :, lanes] = tile

    gather_rows(other_ref, 0, store)
    tokens = left.shape[-1]
    lefts, rights = left[...].reshape(-1, tokens), right_ref[...].reshape(-1, tokens)
    product = lax.dot_general(rights, lefts, (((1,), (1,)), ((), ())), preferred_element_type=F32)
    scatter_rows(product.reshape(right_ref.shape), out_ref)


def whole(shape):
    return pl.BlockSpec(shape, lambda i: (0,) * len(shape))


def layer_of(array, layer):
    return pl.BlockSpec((1, *array.shape[1:]), lambda i: (layer, 0, 0))


HBM = pl.BlockSpec(memory_space=pltpu.HBM)


def call(body, in_specs, out_shapes, scratch, name, flops=None):
    cost = None
    if flops is not None:
        cost = pl.CostEstimate(flops=flops, bytes_accessed=4 * 2**20, transcendentals=2**17)
    return pl.pallas_call(
        body,
        grid=(1,),
        in_specs=in_specs,
        out_specs=[whole(o.shape) for o in out_shapes],
        out_shape=out_shapes,
        scratch_shapes=scratch,
        compiler_params=pltpu.CompilerParams(vmem_limit_bytes=VMEM_LIMIT),
        cost_estimate=cost,
        name=name,
    )


def on_device(chips, pair_field, token_mask, gain, shift, proj_in, gate_in, out_gain, out_shift, gate_out, proj_out):
    tokens = pair_field.shape[0] * pair_field.shape[1]
    channels = pair_field.shape[2]
    pairs = pair_field.reshape(tokens, channels)
    mask_vec = token_mask.reshape(-1, LANES)
    axes = ("h", "x", "z", "y", "core")
    sizes = {axis: lax.axis_size(axis) for axis in axes}
    by_chip = tuple(sizes[axis] for axis in ORDER)
    places = np.arange(2 * chips).reshape([sizes[axis] for axis in axes])
    places = places[:, :, list(Z_LIST)].transpose([axes.index(axis) for axis in (*ORDER, "core")])
    groups = places.reshape(chips, 2).T.tolist()
    n = token_mask.shape[0]
    own_columns = (sizes["z"], 2, 2 * ROWS, n)
    all_columns = (sizes["z"], 2, 2, 2 * ROWS, n)

    shape = jax.ShapeDtypeStruct
    send = shape((chips, 2 * ROWS, LANES), BF)
    sent_by_chip = shape(by_chip + send.shape[1:], BF)
    back = shape((chips, ROWS, LANES), BF)
    back_by_chip = shape(by_chip + back.shape[1:], BF)
    kept = shape((ROWS, LANES, channels), BF)
    kept_wide = shape(kept.shape, F32)
    joined = shape((4 * channels, channels), BF)
    columns = shape((2, 2, channels, LANES), F32)
    rows = shape((ROWS, LANES), F32)
    staged = pltpu.VMEM((channels * 2 * ROWS, LANES), F32)
    wide = pltpu.VMEM((channels * ROWS, LANES), F32)
    own_half = pltpu.VMEM(own_columns, BF)
    total = pltpu.VMEM(all_columns, F32)
    flops = 2 * tokens * channels * channels

    def exchange(x):
        return lax.all_to_all(x, axes, 0, 0, axis_index_groups=groups, tiled=True)

    def triangle(sent, own_call, own_operands, other_call):
        mine = exchange(sent)
        mine, *own_operands = lax.optimization_barrier([mine, *own_operands])
        other = lax.ppermute(mine, "core", [(0, 1), (1, 0)])
        made = own_call(mine.reshape(sent_by_chip.shape), *own_operands)
        other, made = lax.optimization_barrier((other, made))
        result, aside = other_call(other.reshape(sent_by_chip.shape), made)
        return exchange(result.reshape(back.shape)), aside

    sent, normed, weights, vectors = call(
        first_kernel,
        [HBM] * 9,
        [send, kept, rows, rows],
        [
            pltpu.VMEM(pairs.shape, F32),
            pltpu.VMEM(mask_vec.shape, jnp.int32),
            pltpu.SMEM(token_mask.shape, jnp.int32),
            *[pltpu.VMEM(gain.shape, F32)] * 4,
            pltpu.VMEM(proj_in.shape[1:], BF),
            pltpu.VMEM(gate_in.shape[1:], BF),
            staged,
            pltpu.SemaphoreType.DMA((9,)),
        ],
        "project_first",
    )(*(
        pltpu.with_memory_space_constraint(x, pltpu.HBM)
        for x in (pairs, token_mask, mask_vec, gain, shift, out_gain, out_shift, proj_in, gate_in)
    ))

    def outgoing(other, made):
        (result,) = call(
            outgoing_kernel,
            [whole(sent_by_chip.shape), whole(own_columns)],
            [back_by_chip],
            [own_half, own_half, total],
            "outgoing",
        )(other, made[0])
        return result, made[1:]

    combined, (prior, gates, second_weights, column_vectors) = triangle(
        sent,
        call(
            outgoing_own_kernel,
            [
                whole(sent_by_chip.shape), whole(pairs.shape), whole(kept.shape), layer_of(gate_out, 0),
                layer_of(proj_in, 1), layer_of(gate_in, 1), whole(rows.shape),
            ],
            [shape(own_columns, F32), kept_wide, kept_wide, joined, columns],
            [own_half, own_half, total],
            "outgoing_own",
            flops,
        ),
        [pairs, normed, gate_out, proj_in, gate_in, vectors],
        outgoing,
    )
    sent, normed, first_pass = call(
        second_kernel,
        [
            whole(back.shape), whole(kept.shape), whole(kept.shape), whole(joined.shape),
            whole(columns.shape), whole(rows.shape), whole(rows.shape), layer_of(proj_out, 0),
        ],
        [send, kept, kept_wide],
        [staged, wide],
        "finish_and_project",
    )(combined, prior, gates, second_weights, column_vectors, weights, vectors, proj_out)

    def incoming(other, made):
        (result,) = call(
            incoming_kernel,
            [whole(sent_by_chip.shape), whole(own_columns), whole(own_columns)],
            [back_by_chip],
            [pltpu.VMEM(all_columns, BF)],
            "incoming",
        )(other, *made[:2])
        return result, made[2]

    combined, gates = triangle(
        sent,
        call(
            incoming_own_kernel,
            [whole(sent_by_chip.shape), whole(kept.shape), layer_of(gate_out, 1)],
            [shape(own_columns, BF), shape(own_columns, BF), kept_wide],
            [],
            "incoming_own",
            flops,
        ),
        [normed, gate_out],
        incoming,
    )
    (updated,) = call(
        third_kernel,
        [whole(back.shape), whole(kept.shape), whole(kept.shape), whole(columns.shape), layer_of(proj_out, 1)],
        [shape(pairs.shape, F32)],
        [wide],
        "finish",
    )(combined, first_pass, gates, column_vectors, proj_out)
    return updated.reshape(pair_field.shape)


def solution(mesh):
    rows, cols = mesh.devices.shape
    devices = np.asarray(mesh.devices).reshape(2, rows // 2, cols // 4, 2, 2)
    spec = P(("h", "x"), ("z", "y", "core"), None)
    return jax.shard_map(
        functools.partial(on_device, rows * cols // 2),
        mesh=Mesh(devices, ("h", "x", "z", "y", "core")),
        in_specs=(spec,) + (P(),) * 9,
        out_specs=spec,
        check_vma=False,
    )
```

```python
import functools

import jax
import jax.numpy as jnp
import numpy as np
from jax import lax
from jax.experimental import pallas as pl
from jax.experimental.pallas import tpu as pltpu
from jax.sharding import Mesh
from jax.sharding import PartitionSpec as P

EPSILON = 1e-05
ROWS, LANES, HALF = 8, 128, 64
BF, F32 = jnp.bfloat16, jnp.float32
VMEM_LIMIT = 40 * 1024 * 1024
ORDER = ("z", "y", "h", "x")
LISTS = {"z": (6, 2, 7, 3, 0, 4, 1, 5), "y": (0, 1), "h": (1, 0), "x": (2, 3, 0, 1)}


def sigmoid(x):
    return 0.5 * jnp.tanh(0.5 * x) + 0.5


def layer_norm(values, gain, shift, axis):
    average = jnp.mean(values, axis=axis, keepdims=True)
    centred = values - average
    spread = jnp.mean(centred * centred, axis=axis, keepdims=True)
    return centred * lax.rsqrt(spread + EPSILON) * gain + shift


def low_lanes(shape):
    return lax.broadcasted_iota(jnp.int32, shape, len(shape) - 1) < HALF


def swap_halves(first, second):
    low, axis = low_lanes(first.shape), first.ndim - 1
    return (
        jnp.where(low, first, pltpu.roll(second, HALF, axis)),
        jnp.where(low, pltpu.roll(first, HALF, axis), second),
    )


def project(chunk, s, weight, gain, shift, weights, staged, normed_ref):
    normed = layer_norm(chunk, gain, shift, -1).astype(BF)
    normed_ref[s : s + 2] = normed.reshape(2, LANES, LANES)
    both = lax.dot_general(weights, normed, (((1,), (1,)), ((), ())), preferred_element_type=F32)
    halves = sigmoid(both[2 * LANES :]) * both[: 2 * LANES] * weight
    for n in range(2):
        part = halves[:, n * LANES : (n + 1) * LANES]
        staged[pl.ds(s + n, LANES, stride=2 * ROWS), :] = part[:LANES]
        staged[pl.ds(ROWS + s + n, LANES, stride=2 * ROWS), :] = part[LANES:]


def joined_weights(proj_in, gate_in):
    return jnp.concatenate([proj_in.T, gate_in.T], axis=0)


def pair_of(ref, s):
    return ref[s : s + 2].reshape(2 * LANES, LANES)


def residual(prior_ref, gates_ref, proj_out, wide, columns_ref, layer, s):
    parts = [wide[pl.ds(s + n, LANES, stride=ROWS), :] for n in range(2)]
    gain, shift = (jnp.concatenate([columns_ref[layer, n]] * 2, axis=1) for n in range(2))
    mixed = layer_norm(jnp.concatenate(parts, axis=1), gain, shift, 0).astype(BF)
    update = lax.dot_general(mixed, proj_out, (((0,), (0,)), ((), ())), preferred_element_type=F32)
    return pair_of(prior_ref, s) + pair_of(gates_ref, s) * update


def tokens_of(pair_ref, s):
    return jnp.concatenate(
        [pair_ref[pl.ds(b * ROWS + s, HALF, stride=2 * ROWS), :] for b in range(2)], axis=0
    )


def first_kernel(
    pair_hbm, mask_hbm, lanes_hbm, gain_hbm, shift_hbm, out_gain_hbm, out_shift_hbm, proj_hbm, gate_hbm,
    send_ref, normed_ref, weight_ref, vectors_ref,
    pair_ref, mask_vec, mask_smem, gain, shift, out_gain, out_shift, proj_in, gate_in, staged, arrived,
):
    moves = [
        (proj_hbm.at[0], proj_in),
        (gate_hbm.at[0], gate_in),
        (pair_hbm, pair_ref),
        (mask_hbm, mask_smem),
        (lanes_hbm, mask_vec),
        (gain_hbm, gain),
        (shift_hbm, shift),
        (out_gain_hbm, out_gain),
        (out_shift_hbm, out_shift),
    ]
    copies = [
        pltpu.make_async_copy(src, dst, arrived.at[n]) for n, (src, dst) in enumerate(moves)
    ]
    for copy in copies:
        copy.start()
    for copy in copies[:2]:
        copy.wait()
    weights = joined_weights(proj_in[...], gate_in[...])
    for copy in copies[2:]:
        copy.wait()
    row, core = lax.axis_index(("h", "x")), lax.axis_index("core")
    chip = lax.axis_index("z") * 2 + lax.axis_index("y")
    low = low_lanes((1, LANES))
    tokens = mask_vec[pl.ds(row // 2, 1), :].astype(F32)
    own = jnp.where(low == (row % 2 == 0), tokens, pltpu.roll(tokens, HALF, 1))
    begin = (chip * 2 + core) * (2 * ROWS)
    for s in range(0, ROWS, 2):
        both = []
        for n in range(2):
            first = mask_smem[begin + s + n].astype(F32)
            second = mask_smem[begin + ROWS + s + n].astype(F32)
            weight = own * jnp.where(low, first, second)
            weight_ref[pl.ds(s + n, 1), :] = weight
            both.append(weight)
        chunk = jnp.concatenate([tokens_of(pair_ref, s), tokens_of(pair_ref, s + 1)], axis=0)
        weight = jnp.concatenate(both, axis=1)
        project(chunk, s, weight, gain[0:1], shift[0:1], weights, staged, normed_ref)
    send_ref[...] = staged[...].astype(BF).reshape(send_ref.shape)
    for n, ref in enumerate((gain, shift, out_gain, out_shift)):
        vectors_ref[pl.ds(2 * n, 2), :] = ref[...]


def gates_of(normed_ref, gate_out, gates_ref):
    for s in range(0, ROWS, 2):
        gating = jnp.dot(pair_of(normed_ref, s), gate_out[0], preferred_element_type=F32)
        gates_ref[s : s + 2] = sigmoid(gating).reshape(2, LANES, LANES)


def second_kernel(
    back_ref, prior_ref, gates_ref, weights_ref, columns_ref, weight_ref, vectors_ref, proj_out,
    send_ref, normed_ref, pass_ref, staged, wide,
):
    wide[...] = back_ref[...].astype(F32).reshape(wide.shape)
    gain, shift = vectors_ref[pl.ds(1, 1), :], vectors_ref[pl.ds(3, 1), :]
    for s in range(0, ROWS, 2):
        first_pass = residual(prior_ref, gates_ref, proj_out[0], wide, columns_ref, 0, s)
        pass_ref[s : s + 2] = first_pass.reshape(2, LANES, LANES)
        weight = jnp.concatenate([weight_ref[pl.ds(s + n, 1), :] for n in range(2)], axis=1)
        project(first_pass, s, weight, gain, shift, weights_ref[...], staged, normed_ref)
    send_ref[...] = staged[...].astype(BF).reshape(send_ref.shape)


def third_kernel(back_ref, pass_ref, gates_ref, columns_ref, proj_out, out_ref, wide):
    wide[...] = back_ref[...].astype(F32).reshape(wide.shape)
    for s in range(0, ROWS, 2):
        updated = residual(pass_ref, gates_ref, proj_out[0], wide, columns_ref, 1, s)
        for n in range(4):
            place = n % 2 * ROWS + s + n // 2
            out_ref[pl.ds(place, HALF, stride=2 * ROWS), :] = updated[n * HALF : (n + 1) * HALF]


def of_row(row, wide_x):
    at = {"h": LISTS["h"].index(row // wide_x), "x": LISTS["x"].index(row % wide_x)}
    return tuple(at.get(axis, slice(None)) for axis in ORDER)


def columns_first(block):
    if ORDER.index("z") > ORDER.index("y"):
        block = jnp.swapaxes(block, 0, 1)
    zs, ys = ([LISTS[axis].index(n) for n in range(len(LISTS[axis]))] for axis in "zy")
    return jnp.stack([jnp.stack([block[z, y] for y in ys]) for z in zs])


def as_listed(block):
    block = jnp.stack([jnp.stack([block[z, y] for y in LISTS["y"]]) for z in LISTS["z"]])
    return jnp.swapaxes(block, 0, 1) if ORDER.index("z") > ORDER.index("y") else block


def gather_rows(ref, half, store):
    wide_x = ref.shape[ORDER.index("x")]
    rows = slice(half * ROWS, (half + 1) * ROWS)
    for m in range(ROWS // 2):
        first = columns_first(ref[of_row(2 * m, wide_x)].astype(F32))
        second = columns_first(ref[of_row(2 * m + 1, wide_x)].astype(F32))
        low, high = swap_halves(first[:, :, rows], second[:, :, rows])
        store(pl.ds(m * LANES, LANES), jnp.concatenate([low, high], axis=2).astype(BF))


def scatter_rows(product, out_ref):
    wide_x = out_ref.shape[ORDER.index("x")]
    for m in range(ROWS // 2):
        part = product[..., m * LANES : (m + 1) * LANES]
        even, odd = swap_halves(part[:, :, :ROWS], part[:, :, ROWS:])
        out_ref[of_row(2 * m, wide_x)] = as_listed(even.astype(BF))
        out_ref[of_row(2 * m + 1, wide_x)] = as_listed(odd.astype(BF))


def keep_in(ref):
    def store(lanes, tile):
        ref[:, :, :, lanes] = tile

    return store


def outgoing_product(ref, left, right, total):
    gather_rows(ref, 0, keep_in(left))
    gather_rows(ref, 1, keep_in(right))
    tokens = left.shape[-1]
    lefts, rights = left[...].reshape(-1, tokens), right[...].reshape(-1, tokens)
    total[...] = lax.dot_general(
        rights, lefts, (((0,), (0,)), ((), ())), preferred_element_type=F32
    ).reshape(total.shape)
    return total[:, :, lax.axis_index("core")]


def outgoing_own_kernel(
    own_ref, pair_ref, normed_ref, gate_out, proj_in, gate_in, vectors_ref,
    partial_ref, prior_ref, gates_ref, weights_ref, columns_ref, left, right, total,
):
    partial_ref[...] = outgoing_product(own_ref, left, right, total)
    gates_of(normed_ref, gate_out, gates_ref)
    for s in range(ROWS):
        prior_ref[s] = tokens_of(pair_ref, s)
    weights_ref[...] = joined_weights(proj_in[0], gate_in[0])
    for layer in range(2):
        for n in range(2):
            row_vec = vectors_ref[pl.ds(4 + 2 * n + layer, 1), :]
            columns_ref[layer, n] = jnp.broadcast_to(row_vec, (LANES, LANES)).T


def outgoing_kernel(other_ref, partial_ref, out_ref, left, right, total):
    scatter_rows(partial_ref[...] + outgoing_product(other_ref, left, right, total), out_ref)


def incoming_own_kernel(own_ref, normed_ref, gate_out, left_ref, right_ref, gates_ref):
    gather_rows(own_ref, 0, keep_in(left_ref))
    gather_rows(own_ref, 1, keep_in(right_ref))
    gates_of(normed_ref, gate_out, gates_ref)


def incoming_kernel(other_ref, left_ref, right_ref, out_ref, left):
    core = lax.axis_index("core")
    left[:, :, core] = left_ref[...]

    def store(lanes, tile):
        left[:, :, 1 - core, :, lanes] = tile

    gather_rows(other_ref, 0, store)
    tokens = left.shape[-1]
    lefts, rights = left[...].reshape(-1, tokens), right_ref[...].reshape(-1, tokens)
    product = lax.dot_general(rights, lefts, (((1,), (1,)), ((), ())), preferred_element_type=F32)
    scatter_rows(product.reshape(right_ref.shape), out_ref)


def whole(shape):
    return pl.BlockSpec(shape, lambda i: (0,) * len(shape))


def layer_of(array, layer):
    return pl.BlockSpec((1, *array.shape[1:]), lambda i: (layer, 0, 0))


HBM = pl.BlockSpec(memory_space=pltpu.HBM)


def call(body, in_specs, out_shapes, scratch, name, flops=None):
    cost = None
    if flops is not None:
        cost = pl.CostEstimate(flops=flops, bytes_accessed=4 * 2**20, transcendentals=2**17)
    return pl.pallas_call(
        body,
        grid=(1,),
        in_specs=in_specs,
        out_specs=[whole(o.shape) for o in out_shapes],
        out_shape=out_shapes,
        scratch_shapes=scratch,
        compiler_params=pltpu.CompilerParams(vmem_limit_bytes=VMEM_LIMIT),
        cost_estimate=cost,
        name=name,
    )


def on_device(chips, pair_field, token_mask, gain, shift, proj_in, gate_in, out_gain, out_shift, gate_out, proj_out):
    tokens = pair_field.shape[0] * pair_field.shape[1]
    channels = pair_field.shape[2]
    pairs = pair_field.reshape(tokens, channels)
    mask_vec = token_mask.reshape(-1, LANES)
    axes = ("h", "x", "z", "y", "core")
    sizes = {axis: lax.axis_size(axis) for axis in axes}
    by_chip = tuple(sizes[axis] for axis in ORDER)
    places = np.arange(2 * chips).reshape([sizes[axis] for axis in axes])
    places = places[np.ix_(*(LISTS.get(axis, range(2)) for axis in axes))]
    places = places.transpose([axes.index(axis) for axis in (*ORDER, "core")])
    groups = places.reshape(chips, 2).T.tolist()
    n = token_mask.shape[0]
    own_columns = (sizes["z"], 2, 2 * ROWS, n)
    all_columns = (sizes["z"], 2, 2, 2 * ROWS, n)

    shape = jax.ShapeDtypeStruct
    send = shape((chips, 2 * ROWS, LANES), BF)
    sent_by_chip = shape(by_chip + send.shape[1:], BF)
    back = shape((chips, ROWS, LANES), BF)
    back_by_chip = shape(by_chip + back.shape[1:], BF)
    kept = shape((ROWS, LANES, channels), BF)
    kept_wide = shape(kept.shape, F32)
    joined = shape((4 * channels, channels), BF)
    columns = shape((2, 2, channels, LANES), F32)
    rows = shape((ROWS, LANES), F32)
    staged = pltpu.VMEM((channels * 2 * ROWS, LANES), F32)
    wide = pltpu.VMEM((channels * ROWS, LANES), F32)
    own_half = pltpu.VMEM(own_columns, BF)
    total = pltpu.VMEM(all_columns, F32)
    flops = 2 * tokens * channels * channels

    def exchange(x):
        return lax.all_to_all(x, axes, 0, 0, axis_index_groups=groups, tiled=True)

    def triangle(sent, own_call, own_operands, other_call):
        mine = exchange(sent)
        mine, *own_operands = lax.optimization_barrier([mine, *own_operands])
        other = lax.ppermute(mine, "core", [(0, 1), (1, 0)])
        made = own_call(mine.reshape(sent_by_chip.shape), *own_operands)
        other, made = lax.optimization_barrier((other, made))
        result, aside = other_call(other.reshape(sent_by_chip.shape), made)
        return exchange(result.reshape(back.shape)), aside

    sent, normed, weights, vectors = call(
        first_kernel,
        [HBM] * 9,
        [send, kept, rows, rows],
        [
            pltpu.VMEM(pairs.shape, F32),
            pltpu.VMEM(mask_vec.shape, jnp.int32),
            pltpu.SMEM(token_mask.shape, jnp.int32),
            *[pltpu.VMEM(gain.shape, F32)] * 4,
            pltpu.VMEM(proj_in.shape[1:], BF),
            pltpu.VMEM(gate_in.shape[1:], BF),
            staged,
            pltpu.SemaphoreType.DMA((9,)),
        ],
        "project_first",
    )(*(
        pltpu.with_memory_space_constraint(x, pltpu.HBM)
        for x in (pairs, token_mask, mask_vec, gain, shift, out_gain, out_shift, proj_in, gate_in)
    ))

    def outgoing(other, made):
        (result,) = call(
            outgoing_kernel,
            [whole(sent_by_chip.shape), whole(own_columns)],
            [back_by_chip],
            [own_half, own_half, total],
            "outgoing",
        )(other, made[0])
        return result, made[1:]

    combined, (prior, gates, second_weights, column_vectors) = triangle(
        sent,
        call(
            outgoing_own_kernel,
            [
                whole(sent_by_chip.shape), whole(pairs.shape), whole(kept.shape), layer_of(gate_out, 0),
                layer_of(proj_in, 1), layer_of(gate_in, 1), whole(rows.shape),
            ],
            [shape(own_columns, F32), kept_wide, kept_wide, joined, columns],
            [own_half, own_half, total],
            "outgoing_own",
            flops,
        ),
        [pairs, normed, gate_out, proj_in, gate_in, vectors],
        outgoing,
    )
    sent, normed, first_pass = call(
        second_kernel,
        [
            whole(back.shape), whole(kept.shape), whole(kept.shape), whole(joined.shape),
            whole(columns.shape), whole(rows.shape), whole(rows.shape), layer_of(proj_out, 0),
        ],
        [send, kept, kept_wide],
        [staged, wide],
        "finish_and_project",
    )(combined, prior, gates, second_weights, column_vectors, weights, vectors, proj_out)

    def incoming(other, made):
        (result,) = call(
            incoming_kernel,
            [whole(sent_by_chip.shape), whole(own_columns), whole(own_columns)],
            [back_by_chip],
            [pltpu.VMEM(all_columns, BF)],
            "incoming",
        )(other, *made[:2])
        return result, made[2]

    combined, gates = triangle(
        sent,
        call(
            incoming_own_kernel,
            [whole(sent_by_chip.shape), whole(kept.shape), layer_of(gate_out, 1)],
            [shape(own_columns, BF), shape(own_columns, BF), kept_wide],
            [],
            "incoming_own",
            flops,
        ),
        [normed, gate_out],
        incoming,
    )
    (updated,) = call(
        third_kernel,
        [whole(back.shape), whole(kept.shape), whole(kept.shape), whole(columns.shape), layer_of(proj_out, 1)],
        [shape(pairs.shape, F32)],
        [wide],
        "finish",
    )(combined, first_pass, gates, column_vectors, proj_out)
    return updated.reshape(pair_field.shape)


def solution(mesh):
    rows, cols = mesh.devices.shape
    devices = np.asarray(mesh.devices).reshape(2, rows // 2, cols // 4, 2, 2)
    spec = P(("h", "x"), ("z", "y", "core"), None)
    return jax.shard_map(
        functools.partial(on_device, rows * cols // 2),
        mesh=Mesh(devices, ("h", "x", "z", "y", "core")),
        in_specs=(spec,) + (P(),) * 9,
        out_specs=spec,
        check_vma=False,
    )
```

```python
import functools

import jax
import jax.numpy as jnp
import numpy as np
from jax import lax
from jax.experimental import pallas as pl
from jax.experimental.pallas import tpu as pltpu
from jax.sharding import Mesh
from jax.sharding import PartitionSpec as P

EPSILON = 1e-05
ROWS, LANES, HALF = 8, 128, 64
BF, F32 = jnp.bfloat16, jnp.float32
VMEM_LIMIT = 40 * 1024 * 1024
ORDER = ("z", "h", "x", "y")
LISTS = {"z": (6, 2, 7, 3, 0, 4, 1, 5), "y": (0, 1), "h": (1, 0), "x": (2, 3, 0, 1)}


def sigmoid(x):
    return 0.5 * jnp.tanh(0.5 * x) + 0.5


def layer_norm(values, gain, shift, axis):
    average = jnp.mean(values, axis=axis, keepdims=True)
    centred = values - average
    spread = jnp.mean(centred * centred, axis=axis, keepdims=True)
    return centred * lax.rsqrt(spread + EPSILON) * gain + shift


def low_lanes(shape):
    return lax.broadcasted_iota(jnp.int32, shape, len(shape) - 1) < HALF


def swap_halves(first, second):
    low, axis = low_lanes(first.shape), first.ndim - 1
    return (
        jnp.where(low, first, pltpu.roll(second, HALF, axis)),
        jnp.where(low, pltpu.roll(first, HALF, axis), second),
    )


def project(chunk, s, weight, gain, shift, weights, staged, normed_ref):
    normed = layer_norm(chunk, gain, shift, -1).astype(BF)
    normed_ref[s : s + 2] = normed.reshape(2, LANES, LANES)
    both = lax.dot_general(weights, normed, (((1,), (1,)), ((), ())), preferred_element_type=F32)
    halves = sigmoid(both[2 * LANES :]) * both[: 2 * LANES] * weight
    for n in range(2):
        part = halves[:, n * LANES : (n + 1) * LANES]
        staged[pl.ds(s + n, LANES, stride=2 * ROWS), :] = part[:LANES]
        staged[pl.ds(ROWS + s + n, LANES, stride=2 * ROWS), :] = part[LANES:]


def joined_weights(proj_in, gate_in):
    return jnp.concatenate([proj_in.T, gate_in.T], axis=0)


def pair_of(ref, s):
    return ref[s : s + 2].reshape(2 * LANES, LANES)


def residual(prior_ref, gates_ref, proj_out, wide, columns_ref, layer, s):
    parts = [wide[pl.ds(s + n, LANES, stride=ROWS), :] for n in range(2)]
    gain, shift = (jnp.concatenate([columns_ref[layer, n]] * 2, axis=1) for n in range(2))
    mixed = layer_norm(jnp.concatenate(parts, axis=1), gain, shift, 0).astype(BF)
    update = lax.dot_general(mixed, proj_out, (((0,), (0,)), ((), ())), preferred_element_type=F32)
    return pair_of(prior_ref, s) + pair_of(gates_ref, s) * update


def tokens_of(pair_ref, s):
    return jnp.concatenate(
        [pair_ref[pl.ds(b * ROWS + s, HALF, stride=2 * ROWS), :] for b in range(2)], axis=0
    )


def first_kernel(
    pair_hbm, mask_hbm, lanes_hbm, gain_hbm, shift_hbm, out_gain_hbm, out_shift_hbm, proj_hbm, gate_hbm,
    send_ref, normed_ref, weight_ref, vectors_ref,
    pair_ref, mask_vec, mask_smem, gain, shift, out_gain, out_shift, proj_in, gate_in, staged, arrived,
):
    moves = [
        (proj_hbm.at[0], proj_in),
        (gate_hbm.at[0], gate_in),
        (pair_hbm, pair_ref),
        (mask_hbm, mask_smem),
        (lanes_hbm, mask_vec),
        (gain_hbm, gain),
        (shift_hbm, shift),
        (out_gain_hbm, out_gain),
        (out_shift_hbm, out_shift),
    ]
    copies = [
        pltpu.make_async_copy(src, dst, arrived.at[n]) for n, (src, dst) in enumerate(moves)
    ]
    for copy in copies:
        copy.start()
    for copy in copies[:2]:
        copy.wait()
    weights = joined_weights(proj_in[...], gate_in[...])
    for copy in copies[2:]:
        copy.wait()
    row, core = lax.axis_index(("h", "x")), lax.axis_index("core")
    chip = lax.axis_index("z") * 2 + lax.axis_index("y")
    low = low_lanes((1, LANES))
    tokens = mask_vec[pl.ds(row // 2, 1), :].astype(F32)
    own = jnp.where(low == (row % 2 == 0), tokens, pltpu.roll(tokens, HALF, 1))
    begin = (chip * 2 + core) * (2 * ROWS)
    for s in range(0, ROWS, 2):
        both = []
        for n in range(2):
            first = mask_smem[begin + s + n].astype(F32)
            second = mask_smem[begin + ROWS + s + n].astype(F32)
            weight = own * jnp.where(low, first, second)
            weight_ref[pl.ds(s + n, 1), :] = weight
            both.append(weight)
        chunk = jnp.concatenate([tokens_of(pair_ref, s), tokens_of(pair_ref, s + 1)], axis=0)
        weight = jnp.concatenate(both, axis=1)
        project(chunk, s, weight, gain[0:1], shift[0:1], weights, staged, normed_ref)
    send_ref[...] = staged[...].astype(BF).reshape(send_ref.shape)
    for n, ref in enumerate((gain, shift, out_gain, out_shift)):
        vectors_ref[pl.ds(2 * n, 2), :] = ref[...]


def gates_of(normed_ref, gate_out, gates_ref):
    for s in range(0, ROWS, 2):
        gating = jnp.dot(pair_of(normed_ref, s), gate_out[0], preferred_element_type=F32)
        gates_ref[s : s + 2] = sigmoid(gating).reshape(2, LANES, LANES)


def second_kernel(
    back_ref, prior_ref, gates_ref, weights_ref, columns_ref, weight_ref, vectors_ref, proj_out,
    send_ref, normed_ref, pass_ref, staged, wide,
):
    wide[...] = back_ref[...].astype(F32).reshape(wide.shape)
    gain, shift = vectors_ref[pl.ds(1, 1), :], vectors_ref[pl.ds(3, 1), :]
    for s in range(0, ROWS, 2):
        first_pass = residual(prior_ref, gates_ref, proj_out[0], wide, columns_ref, 0, s)
        pass_ref[s : s + 2] = first_pass.reshape(2, LANES, LANES)
        weight = jnp.concatenate([weight_ref[pl.ds(s + n, 1), :] for n in range(2)], axis=1)
        project(first_pass, s, weight, gain, shift, weights_ref[...], staged, normed_ref)
    send_ref[...] = staged[...].astype(BF).reshape(send_ref.shape)


def third_kernel(back_ref, pass_ref, gates_ref, columns_ref, proj_out, out_ref, wide):
    wide[...] = back_ref[...].astype(F32).reshape(wide.shape)
    for s in range(0, ROWS, 2):
        updated = residual(pass_ref, gates_ref, proj_out[0], wide, columns_ref, 1, s)
        for n in range(4):
            place = n % 2 * ROWS + s + n // 2
            out_ref[pl.ds(place, HALF, stride=2 * ROWS), :] = updated[n * HALF : (n + 1) * HALF]


def of_row(row, wide_x):
    at = {"h": LISTS["h"].index(row // wide_x), "x": LISTS["x"].index(row % wide_x)}
    return tuple(at.get(axis, slice(None)) for axis in ORDER)


def columns_first(block):
    if ORDER.index("z") > ORDER.index("y"):
        block = jnp.swapaxes(block, 0, 1)
    zs, ys = ([LISTS[axis].index(n) for n in range(len(LISTS[axis]))] for axis in "zy")
    return jnp.stack([jnp.stack([block[z, y] for y in ys]) for z in zs])


def as_listed(block):
    block = jnp.stack([jnp.stack([block[z, y] for y in LISTS["y"]]) for z in LISTS["z"]])
    return jnp.swapaxes(block, 0, 1) if ORDER.index("z") > ORDER.index("y") else block


def gather_rows(ref, half, store):
    wide_x = ref.shape[ORDER.index("x")]
    rows = slice(half * ROWS, (half + 1) * ROWS)
    for m in range(ROWS // 2):
        first = columns_first(ref[of_row(2 * m, wide_x)].astype(F32))
        second = columns_first(ref[of_row(2 * m + 1, wide_x)].astype(F32))
        low, high = swap_halves(first[:, :, rows], second[:, :, rows])
        store(pl.ds(m * LANES, LANES), jnp.concatenate([low, high], axis=2).astype(BF))


def scatter_rows(product, out_ref):
    wide_x = out_ref.shape[ORDER.index("x")]
    for m in range(ROWS // 2):
        part = product[..., m * LANES : (m + 1) * LANES]
        even, odd = swap_halves(part[:, :, :ROWS], part[:, :, ROWS:])
        out_ref[of_row(2 * m, wide_x)] = as_listed(even.astype(BF))
        out_ref[of_row(2 * m + 1, wide_x)] = as_listed(odd.astype(BF))


def keep_in(ref):
    def store(lanes, tile):
        ref[:, :, :, lanes] = tile

    return store


def outgoing_product(ref, left, right, total):
    gather_rows(ref, 0, keep_in(left))
    gather_rows(ref, 1, keep_in(right))
    tokens = left.shape[-1]
    lefts, rights = left[...].reshape(-1, tokens), right[...].reshape(-1, tokens)
    total[...] = lax.dot_general(
        rights, lefts, (((0,), (0,)), ((), ())), preferred_element_type=F32
    ).reshape(total.shape)
    return total[:, :, lax.axis_index("core")]


def outgoing_own_kernel(
    own_ref, pair_ref, normed_ref, gate_out, proj_in, gate_in, vectors_ref,
    partial_ref, prior_ref, gates_ref, weights_ref, columns_ref, left, right, total,
):
    partial_ref[...] = outgoing_product(own_ref, left, right, total)
    gates_of(normed_ref, gate_out, gates_ref)
    for s in range(ROWS):
        prior_ref[s] = tokens_of(pair_ref, s)
    weights_ref[...] = joined_weights(proj_in[0], gate_in[0])
    for layer in range(2):
        for n in range(2):
            row_vec = vectors_ref[pl.ds(4 + 2 * n + layer, 1), :]
            columns_ref[layer, n] = jnp.broadcast_to(row_vec, (LANES, LANES)).T


def outgoing_kernel(other_ref, partial_ref, out_ref, left, right, total):
    scatter_rows(partial_ref[...] + outgoing_product(other_ref, left, right, total), out_ref)


def incoming_left_kernel(own_ref, left_ref):
    gather_rows(own_ref, 0, keep_in(left_ref))


def incoming_right_kernel(own_ref, normed_ref, gate_out, right_ref, gates_ref):
    gather_rows(own_ref, 1, keep_in(right_ref))
    gates_of(normed_ref, gate_out, gates_ref)


def incoming_kernel(left_ref, other_ref, right_ref, out_ref, left):
    core = lax.axis_index("core")
    left[:, :, core] = left_ref[...]
    left[:, :, 1 - core] = other_ref[...]
    tokens = left.shape[-1]
    lefts, rights = left[...].reshape(-1, tokens), right_ref[...].reshape(-1, tokens)
    product = lax.dot_general(rights, lefts, (((1,), (1,)), ((), ())), preferred_element_type=F32)
    scatter_rows(product.reshape(right_ref.shape), out_ref)


def whole(shape):
    return pl.BlockSpec(shape, lambda i: (0,) * len(shape))


def layer_of(array, layer):
    return pl.BlockSpec((1, *array.shape[1:]), lambda i: (layer, 0, 0))


HBM = pl.BlockSpec(memory_space=pltpu.HBM)


def call(body, in_specs, out_shapes, scratch, name, flops=None):
    cost = None
    if flops is not None:
        cost = pl.CostEstimate(flops=flops, bytes_accessed=4 * 2**20, transcendentals=2**17)
    return pl.pallas_call(
        body,
        grid=(1,),
        in_specs=in_specs,
        out_specs=[whole(o.shape) for o in out_shapes],
        out_shape=out_shapes,
        scratch_shapes=scratch,
        compiler_params=pltpu.CompilerParams(vmem_limit_bytes=VMEM_LIMIT),
        cost_estimate=cost,
        name=name,
    )


def on_device(chips, pair_field, token_mask, gain, shift, proj_in, gate_in, out_gain, out_shift, gate_out, proj_out):
    tokens = pair_field.shape[0] * pair_field.shape[1]
    channels = pair_field.shape[2]
    pairs = pair_field.reshape(tokens, channels)
    mask_vec = token_mask.reshape(-1, LANES)
    axes = ("h", "x", "z", "y", "core")
    sizes = {axis: lax.axis_size(axis) for axis in axes}
    by_chip = tuple(sizes[axis] for axis in ORDER)
    places = np.arange(2 * chips).reshape([sizes[axis] for axis in axes])
    places = places[np.ix_(*(LISTS.get(axis, range(2)) for axis in axes))]
    places = places.transpose([axes.index(axis) for axis in (*ORDER, "core")])
    groups = places.reshape(chips, 2).T.tolist()
    n = token_mask.shape[0]
    own_columns = (sizes["z"], 2, 2 * ROWS, n)
    all_columns = (sizes["z"], 2, 2, 2 * ROWS, n)

    shape = jax.ShapeDtypeStruct
    send = shape((chips, 2 * ROWS, LANES), BF)
    sent_by_chip = shape(by_chip + send.shape[1:], BF)
    back = shape((chips, ROWS, LANES), BF)
    back_by_chip = shape(by_chip + back.shape[1:], BF)
    kept = shape((ROWS, LANES, channels), BF)
    kept_wide = shape(kept.shape, F32)
    joined = shape((4 * channels, channels), BF)
    columns = shape((2, 2, channels, LANES), F32)
    rows = shape((ROWS, LANES), F32)
    staged = pltpu.VMEM((channels * 2 * ROWS, LANES), F32)
    wide = pltpu.VMEM((channels * ROWS, LANES), F32)
    own_half = pltpu.VMEM(own_columns, BF)
    total = pltpu.VMEM(all_columns, F32)
    flops = 2 * tokens * channels * channels

    def exchange(x):
        return lax.all_to_all(x, axes, 0, 0, axis_index_groups=groups, tiled=True)

    def swap_cores(x):
        return lax.ppermute(x, "core", [(0, 1), (1, 0)])

    sent, normed, weights, vectors = call(
        first_kernel,
        [HBM] * 9,
        [send, kept, rows, rows],
        [
            pltpu.VMEM(pairs.shape, F32),
            pltpu.VMEM(mask_vec.shape, jnp.int32),
            pltpu.SMEM(token_mask.shape, jnp.int32),
            *[pltpu.VMEM(gain.shape, F32)] * 4,
            pltpu.VMEM(proj_in.shape[1:], BF),
            pltpu.VMEM(gate_in.shape[1:], BF),
            staged,
            pltpu.SemaphoreType.DMA((9,)),
        ],
        "project_first",
    )(*(
        pltpu.with_memory_space_constraint(x, pltpu.HBM)
        for x in (pairs, token_mask, mask_vec, gain, shift, out_gain, out_shift, proj_in, gate_in)
    ))

    mine, pairs, normed = lax.optimization_barrier((exchange(sent), pairs, normed))
    other = swap_cores(mine)
    made = call(
        outgoing_own_kernel,
        [
            whole(sent_by_chip.shape), whole(pairs.shape), whole(kept.shape), layer_of(gate_out, 0),
            layer_of(proj_in, 1), layer_of(gate_in, 1), whole(rows.shape),
        ],
        [shape(own_columns, F32), kept_wide, kept_wide, joined, columns],
        [own_half, own_half, total],
        "outgoing_own",
        flops,
    )(mine.reshape(sent_by_chip.shape), pairs, normed, gate_out, proj_in, gate_in, vectors)
    other, (partial, prior, gates, second_weights, column_vectors) = lax.optimization_barrier((other, made))
    (result,) = call(
        outgoing_kernel,
        [whole(sent_by_chip.shape), whole(own_columns)],
        [back_by_chip],
        [own_half, own_half, total],
        "outgoing",
    )(other.reshape(sent_by_chip.shape), partial)
    combined = exchange(result.reshape(back.shape))
    sent, normed, first_pass = call(
        second_kernel,
        [
            whole(back.shape), whole(kept.shape), whole(kept.shape), whole(joined.shape),
            whole(columns.shape), whole(rows.shape), whole(rows.shape), layer_of(proj_out, 0),
        ],
        [send, kept, kept_wide],
        [staged, wide],
        "finish_and_project",
    )(combined, prior, gates, second_weights, column_vectors, weights, vectors, proj_out)

    mine, normed = lax.optimization_barrier((exchange(sent).reshape(sent_by_chip.shape), normed))
    (left,) = call(
        incoming_left_kernel,
        [whole(sent_by_chip.shape)],
        [shape(own_columns, BF)],
        [],
        "incoming_left",
    )(mine)
    mine, left, normed = lax.optimization_barrier((mine, left, normed))
    other = swap_cores(left)
    made = call(
        incoming_right_kernel,
        [whole(sent_by_chip.shape), whole(kept.shape), layer_of(gate_out, 1)],
        [shape(own_columns, BF), kept_wide],
        [],
        "incoming_right",
        flops,
    )(mine, normed, gate_out)
    other, (right, gates) = lax.optimization_barrier((other, made))
    (result,) = call(
        incoming_kernel,
        [whole(own_columns)] * 3,
        [back_by_chip],
        [pltpu.VMEM(all_columns, BF)],
        "incoming",
    )(left, other, right)
    combined = exchange(result.reshape(back.shape))
    (updated,) = call(
        third_kernel,
        [whole(back.shape), whole(kept.shape), whole(kept.shape), whole(columns.shape), layer_of(proj_out, 1)],
        [shape(pairs.shape, F32)],
        [wide],
        "finish",
    )(combined, first_pass, gates, column_vectors, proj_out)
    return updated.reshape(pair_field.shape)


def solution(mesh):
    rows, cols = mesh.devices.shape
    devices = np.asarray(mesh.devices).reshape(2, rows // 2, cols // 4, 2, 2)
    spec = P(("h", "x"), ("z", "y", "core"), None)
    return jax.shard_map(
        functools.partial(on_device, rows * cols // 2),
        mesh=Mesh(devices, ("h", "x", "z", "y", "core")),
        in_specs=(spec,) + (P(),) * 9,
        out_specs=spec,
        check_vma=False,
    )
```

```python
import functools

import jax
import jax.numpy as jnp
import numpy as np
from jax import lax
from jax.experimental import pallas as pl
from jax.experimental.pallas import tpu as pltpu
from jax.sharding import Mesh
from jax.sharding import PartitionSpec as P

EPSILON = 1e-05
ROWS, LANES, HALF = 8, 128, 64
BF, F32 = jnp.bfloat16, jnp.float32
VMEM_LIMIT = 40 * 1024 * 1024
ORDER = ("z", "h", "x", "y")
LISTS = {"z": (5, 1, 6, 2, 7, 3, 0, 4), "y": (0, 1), "h": (1, 0), "x": (2, 3, 0, 1)}


def sigmoid(x):
    return 0.5 * jnp.tanh(0.5 * x) + 0.5


def layer_norm(values, gain, shift, axis):
    average = jnp.mean(values, axis=axis, keepdims=True)
    centred = values - average
    spread = jnp.mean(centred * centred, axis=axis, keepdims=True)
    return centred * lax.rsqrt(spread + EPSILON) * gain + shift


def low_lanes(shape):
    return lax.broadcasted_iota(jnp.int32, shape, len(shape) - 1) < HALF


def swap_halves(first, second):
    low, axis = low_lanes(first.shape), first.ndim - 1
    return (
        jnp.where(low, first, pltpu.roll(second, HALF, axis)),
        jnp.where(low, pltpu.roll(first, HALF, axis), second),
    )


def project(chunk, s, weight, gain, shift, weights, staged, normed_ref):
    normed = layer_norm(chunk, gain, shift, -1).astype(BF)
    normed_ref[s : s + 2] = normed.reshape(2, LANES, LANES)
    both = lax.dot_general(weights, normed, (((1,), (1,)), ((), ())), preferred_element_type=F32)
    halves = sigmoid(both[2 * LANES :]) * both[: 2 * LANES] * weight
    for n in range(2):
        part = halves[:, n * LANES : (n + 1) * LANES]
        staged[pl.ds(s + n, LANES, stride=2 * ROWS), :] = part[:LANES]
        staged[pl.ds(ROWS + s + n, LANES, stride=2 * ROWS), :] = part[LANES:]


def joined_weights(proj_in, gate_in):
    return jnp.concatenate([proj_in.T, gate_in.T], axis=0)


def pair_of(ref, s):
    return ref[s : s + 2].reshape(2 * LANES, LANES)


def residual(prior_ref, gates_ref, proj_out, wide, columns_ref, layer, s):
    parts = [wide[pl.ds(s + n, LANES, stride=ROWS), :] for n in range(2)]
    gain, shift = (jnp.concatenate([columns_ref[layer, n]] * 2, axis=1) for n in range(2))
    mixed = layer_norm(jnp.concatenate(parts, axis=1), gain, shift, 0).astype(BF)
    update = lax.dot_general(mixed, proj_out, (((0,), (0,)), ((), ())), preferred_element_type=F32)
    return pair_of(prior_ref, s) + pair_of(gates_ref, s) * update


def tokens_of(pair_ref, s):
    return jnp.concatenate(
        [pair_ref[pl.ds(b * ROWS + s, HALF, stride=2 * ROWS), :] for b in range(2)], axis=0
    )


def first_kernel(
    pair_hbm, mask_hbm, lanes_hbm, gain_hbm, shift_hbm, out_gain_hbm, out_shift_hbm, proj_hbm, gate_hbm,
    send_ref, normed_ref, weight_ref, vectors_ref,
    pair_ref, mask_vec, mask_smem, gain, shift, out_gain, out_shift, proj_in, gate_in, staged, arrived,
):
    moves = [
        (proj_hbm.at[0], proj_in),
        (gate_hbm.at[0], gate_in),
        (pair_hbm, pair_ref),
        (mask_hbm, mask_smem),
        (lanes_hbm, mask_vec),
        (gain_hbm, gain),
        (shift_hbm, shift),
        (out_gain_hbm, out_gain),
        (out_shift_hbm, out_shift),
    ]
    copies = [
        pltpu.make_async_copy(src, dst, arrived.at[n]) for n, (src, dst) in enumerate(moves)
    ]
    for copy in copies:
        copy.start()
    for copy in copies[:2]:
        copy.wait()
    weights = joined_weights(proj_in[...], gate_in[...])
    for copy in copies[2:]:
        copy.wait()
    row, core = lax.axis_index(("h", "x")), lax.axis_index("core")
    chip = lax.axis_index("z") * 2 + lax.axis_index("y")
    low = low_lanes((1, LANES))
    tokens = mask_vec[pl.ds(row // 2, 1), :].astype(F32)
    own = jnp.where(low == (row % 2 == 0), tokens, pltpu.roll(tokens, HALF, 1))
    begin = (chip * 2 + core) * (2 * ROWS)
    for s in range(0, ROWS, 2):
        both = []
        for n in range(2):
            first = mask_smem[begin + s + n].astype(F32)
            second = mask_smem[begin + ROWS + s + n].astype(F32)
            weight = own * jnp.where(low, first, second)
            weight_ref[pl.ds(s + n, 1), :] = weight
            both.append(weight)
        chunk = jnp.concatenate([tokens_of(pair_ref, s), tokens_of(pair_ref, s + 1)], axis=0)
        weight = jnp.concatenate(both, axis=1)
        project(chunk, s, weight, gain[0:1], shift[0:1], weights, staged, normed_ref)
    send_ref[...] = staged[...].astype(BF).reshape(send_ref.shape)
    for n, ref in enumerate((gain, shift, out_gain, out_shift)):
        vectors_ref[pl.ds(2 * n, 2), :] = ref[...]


def gates_of(normed_ref, gate_out, gates_ref):
    for s in range(0, ROWS, 2):
        gating = jnp.dot(pair_of(normed_ref, s), gate_out[0], preferred_element_type=F32)
        gates_ref[s : s + 2] = sigmoid(gating).reshape(2, LANES, LANES)


def second_kernel(
    back_ref, prior_ref, gates_ref, weights_ref, columns_ref, weight_ref, vectors_ref, proj_out,
    send_ref, normed_ref, pass_ref, staged, wide,
):
    wide[...] = back_ref[...].astype(F32).reshape(wide.shape)
    gain, shift = vectors_ref[pl.ds(1, 1), :], vectors_ref[pl.ds(3, 1), :]
    for s in range(0, ROWS, 2):
        first_pass = residual(prior_ref, gates_ref, proj_out[0], wide, columns_ref, 0, s)
        pass_ref[s : s + 2] = first_pass.reshape(2, LANES, LANES)
        weight = jnp.concatenate([weight_ref[pl.ds(s + n, 1), :] for n in range(2)], axis=1)
        project(first_pass, s, weight, gain, shift, weights_ref[...], staged, normed_ref)
    send_ref[...] = staged[...].astype(BF).reshape(send_ref.shape)


def third_kernel(back_ref, pass_ref, gates_ref, columns_ref, proj_out, out_ref, wide):
    wide[...] = back_ref[...].astype(F32).reshape(wide.shape)
    for s in range(0, ROWS, 2):
        updated = residual(pass_ref, gates_ref, proj_out[0], wide, columns_ref, 1, s)
        for n in range(4):
            place = n % 2 * ROWS + s + n // 2
            out_ref[pl.ds(place, HALF, stride=2 * ROWS), :] = updated[n * HALF : (n + 1) * HALF]


def of_row(row, wide_x):
    at = {"h": LISTS["h"].index(row // wide_x), "x": LISTS["x"].index(row % wide_x)}
    return tuple(at.get(axis, slice(None)) for axis in ORDER)


def columns_first(block):
    if ORDER.index("z") > ORDER.index("y"):
        block = jnp.swapaxes(block, 0, 1)
    zs, ys = ([LISTS[axis].index(n) for n in range(len(LISTS[axis]))] for axis in "zy")
    return jnp.stack([jnp.stack([block[z, y] for y in ys]) for z in zs])


def as_listed(block):
    block = jnp.stack([jnp.stack([block[z, y] for y in LISTS["y"]]) for z in LISTS["z"]])
    return jnp.swapaxes(block, 0, 1) if ORDER.index("z") > ORDER.index("y") else block


def gather_rows(ref, half, store):
    wide_x = ref.shape[ORDER.index("x")]
    rows = slice(half * ROWS, (half + 1) * ROWS)
    for m in range(ROWS // 2):
        first = columns_first(ref[of_row(2 * m, wide_x)].astype(F32))
        second = columns_first(ref[of_row(2 * m + 1, wide_x)].astype(F32))
        low, high = swap_halves(first[:, :, rows], second[:, :, rows])
        store(pl.ds(m * LANES, LANES), jnp.concatenate([low, high], axis=2).astype(BF))


def scatter_rows(product, out_ref):
    wide_x = out_ref.shape[ORDER.index("x")]
    for m in range(ROWS // 2):
        part = product[..., m * LANES : (m + 1) * LANES]
        even, odd = swap_halves(part[:, :, :ROWS], part[:, :, ROWS:])
        out_ref[of_row(2 * m, wide_x)] = as_listed(even.astype(BF))
        out_ref[of_row(2 * m + 1, wide_x)] = as_listed(odd.astype(BF))


def keep_in(ref):
    def store(lanes, tile):
        ref[:, :, :, lanes] = tile

    return store


def outgoing_product(ref, left, right, total):
    gather_rows(ref, 0, keep_in(left))
    gather_rows(ref, 1, keep_in(right))
    tokens = left.shape[-1]
    lefts, rights = left[...].reshape(-1, tokens), right[...].reshape(-1, tokens)
    total[...] = lax.dot_general(
        rights, lefts, (((0,), (0,)), ((), ())), preferred_element_type=F32
    ).reshape(total.shape)
    return total[:, :, lax.axis_index("core")]


def outgoing_own_kernel(
    own_ref, pair_ref, normed_ref, gate_out, proj_in, gate_in, vectors_ref,
    partial_ref, prior_ref, gates_ref, weights_ref, columns_ref, left, right, total,
):
    partial_ref[...] = outgoing_product(own_ref, left, right, total)
    gates_of(normed_ref, gate_out, gates_ref)
    for s in range(ROWS):
        prior_ref[s] = tokens_of(pair_ref, s)
    weights_ref[...] = joined_weights(proj_in[0], gate_in[0])
    for layer in range(2):
        for n in range(2):
            row_vec = vectors_ref[pl.ds(4 + 2 * n + layer, 1), :]
            columns_ref[layer, n] = jnp.broadcast_to(row_vec, (LANES, LANES)).T


def outgoing_kernel(other_ref, partial_ref, out_ref, left, right, total):
    scatter_rows(partial_ref[...] + outgoing_product(other_ref, left, right, total), out_ref)


def incoming_left_kernel(own_ref, left_ref):
    gather_rows(own_ref, 0, keep_in(left_ref))


def incoming_right_kernel(own_ref, normed_ref, gate_out, right_ref, gates_ref):
    gather_rows(own_ref, 1, keep_in(right_ref))
    gates_of(normed_ref, gate_out, gates_ref)


def incoming_kernel(left_ref, other_ref, right_ref, out_ref, left):
    core = lax.axis_index("core")
    left[:, :, core] = left_ref[...]
    left[:, :, 1 - core] = other_ref[...]
    tokens = left.shape[-1]
    lefts, rights = left[...].reshape(-1, tokens), right_ref[...].reshape(-1, tokens)
    product = lax.dot_general(rights, lefts, (((1,), (1,)), ((), ())), preferred_element_type=F32)
    scatter_rows(product.reshape(right_ref.shape), out_ref)


def whole(shape):
    return pl.BlockSpec(shape, lambda i: (0,) * len(shape))


def layer_of(array, layer):
    return pl.BlockSpec((1, *array.shape[1:]), lambda i: (layer, 0, 0))


HBM = pl.BlockSpec(memory_space=pltpu.HBM)


def call(body, in_specs, out_shapes, scratch, name, flops=None):
    cost = None
    if flops is not None:
        cost = pl.CostEstimate(flops=flops, bytes_accessed=4 * 2**20, transcendentals=2**17)
    return pl.pallas_call(
        body,
        grid=(1,),
        in_specs=in_specs,
        out_specs=[whole(o.shape) for o in out_shapes],
        out_shape=out_shapes,
        scratch_shapes=scratch,
        compiler_params=pltpu.CompilerParams(vmem_limit_bytes=VMEM_LIMIT),
        cost_estimate=cost,
        name=name,
    )


def on_device(chips, pair_field, token_mask, gain, shift, proj_in, gate_in, out_gain, out_shift, gate_out, proj_out):
    tokens = pair_field.shape[0] * pair_field.shape[1]
    channels = pair_field.shape[2]
    pairs = pair_field.reshape(tokens, channels)
    mask_vec = token_mask.reshape(-1, LANES)
    axes = ("h", "x", "z", "y", "core")
    sizes = {axis: lax.axis_size(axis) for axis in axes}
    by_chip = tuple(sizes[axis] for axis in ORDER)
    places = np.arange(2 * chips).reshape([sizes[axis] for axis in axes])
    places = places[np.ix_(*(LISTS.get(axis, range(2)) for axis in axes))]
    places = places.transpose([axes.index(axis) for axis in (*ORDER, "core")])
    groups = places.reshape(chips, 2).T.tolist()
    n = token_mask.shape[0]
    own_columns = (sizes["z"], 2, 2 * ROWS, n)
    all_columns = (sizes["z"], 2, 2, 2 * ROWS, n)

    shape = jax.ShapeDtypeStruct
    send = shape((chips, 2 * ROWS, LANES), BF)
    sent_by_chip = shape(by_chip + send.shape[1:], BF)
    back = shape((chips, ROWS, LANES), BF)
    back_by_chip = shape(by_chip + back.shape[1:], BF)
    kept = shape((ROWS, LANES, channels), BF)
    kept_wide = shape(kept.shape, F32)
    joined = shape((4 * channels, channels), BF)
    columns = shape((2, 2, channels, LANES), F32)
    rows = shape((ROWS, LANES), F32)
    staged = pltpu.VMEM((channels * 2 * ROWS, LANES), F32)
    wide = pltpu.VMEM((channels * ROWS, LANES), F32)
    own_half = pltpu.VMEM(own_columns, BF)
    total = pltpu.VMEM(all_columns, F32)
    flops = 2 * tokens * channels * channels

    def exchange(x):
        return lax.all_to_all(x, axes, 0, 0, axis_index_groups=groups, tiled=True)

    def swap_cores(x):
        return lax.ppermute(x, "core", [(0, 1), (1, 0)])

    sent, normed, weights, vectors = call(
        first_kernel,
        [HBM] * 9,
        [send, kept, rows, rows],
        [
            pltpu.VMEM(pairs.shape, F32),
            pltpu.VMEM(mask_vec.shape, jnp.int32),
            pltpu.SMEM(token_mask.shape, jnp.int32),
            *[pltpu.VMEM(gain.shape, F32)] * 4,
            pltpu.VMEM(proj_in.shape[1:], BF),
            pltpu.VMEM(gate_in.shape[1:], BF),
            staged,
            pltpu.SemaphoreType.DMA((9,)),
        ],
        "project_first",
    )(*(
        pltpu.with_memory_space_constraint(x, pltpu.HBM)
        for x in (pairs, token_mask, mask_vec, gain, shift, out_gain, out_shift, proj_in, gate_in)
    ))

    mine, pairs, normed = lax.optimization_barrier((exchange(sent), pairs, normed))
    other = swap_cores(mine)
    made = call(
        outgoing_own_kernel,
        [
            whole(sent_by_chip.shape), whole(pairs.shape), whole(kept.shape), layer_of(gate_out, 0),
            layer_of(proj_in, 1), layer_of(gate_in, 1), whole(rows.shape),
        ],
        [shape(own_columns, F32), kept_wide, kept_wide, joined, columns],
        [own_half, own_half, total],
        "outgoing_own",
        flops,
    )(mine.reshape(sent_by_chip.shape), pairs, normed, gate_out, proj_in, gate_in, vectors)
    other, (partial, prior, gates, second_weights, column_vectors) = lax.optimization_barrier((other, made))
    (result,) = call(
        outgoing_kernel,
        [whole(sent_by_chip.shape), whole(own_columns)],
        [back_by_chip],
        [own_half, own_half, total],
        "outgoing",
    )(other.reshape(sent_by_chip.shape), partial)
    combined = exchange(result.reshape(back.shape))
    sent, normed, first_pass = call(
        second_kernel,
        [
            whole(back.shape), whole(kept.shape), whole(kept.shape), whole(joined.shape),
            whole(columns.shape), whole(rows.shape), whole(rows.shape), layer_of(proj_out, 0),
        ],
        [send, kept, kept_wide],
        [staged, wide],
        "finish_and_project",
    )(combined, prior, gates, second_weights, column_vectors, weights, vectors, proj_out)

    mine, normed = lax.optimization_barrier((exchange(sent).reshape(sent_by_chip.shape), normed))
    (left,) = call(
        incoming_left_kernel,
        [whole(sent_by_chip.shape)],
        [shape(own_columns, BF)],
        [],
        "incoming_left",
    )(mine)
    mine, left, normed = lax.optimization_barrier((mine, left, normed))
    other = swap_cores(left)
    made = call(
        incoming_right_kernel,
        [whole(sent_by_chip.shape), whole(kept.shape), layer_of(gate_out, 1)],
        [shape(own_columns, BF), kept_wide],
        [],
        "incoming_right",
        flops,
    )(mine, normed, gate_out)
    other, (right, gates) = lax.optimization_barrier((other, made))
    (result,) = call(
        incoming_kernel,
        [whole(own_columns)] * 3,
        [back_by_chip],
        [pltpu.VMEM(all_columns, BF)],
        "incoming",
    )(left, other, right)
    combined = exchange(result.reshape(back.shape))
    (updated,) = call(
        third_kernel,
        [whole(back.shape), whole(kept.shape), whole(kept.shape), whole(columns.shape), layer_of(proj_out, 1)],
        [shape(pairs.shape, F32)],
        [wide],
        "finish",
    )(combined, first_pass, gates, column_vectors, proj_out)
    return updated.reshape(pair_field.shape)


def solution(mesh):
    rows, cols = mesh.devices.shape
    devices = np.asarray(mesh.devices).reshape(2, rows // 2, cols // 4, 2, 2)
    spec = P(("h", "x"), ("z", "y", "core"), None)
    return jax.shard_map(
        functools.partial(on_device, rows * cols // 2),
        mesh=Mesh(devices, ("h", "x", "z", "y", "core")),
        in_specs=(spec,) + (P(),) * 9,
        out_specs=spec,
        check_vma=False,
    )
```

```python
import functools

import jax
import jax.numpy as jnp
import numpy as np
from jax import lax
from jax.experimental import pallas as pl
from jax.experimental.pallas import tpu as pltpu
from jax.sharding import Mesh
from jax.sharding import PartitionSpec as P

EPSILON = 1e-05
ROWS, LANES, HALF = 8, 128, 64
BF, F32 = jnp.bfloat16, jnp.float32
VMEM_LIMIT = 40 * 1024 * 1024
ORDER = ("z", "h", "x", "y")
LISTS = {"z": (5, 1, 6, 2, 7, 3, 0, 4), "y": (0, 1), "h": (1, 0), "x": (2, 3, 0, 1)}


def sigmoid(x):
    return 0.5 * jnp.tanh(0.5 * x) + 0.5


def layer_norm(values, gain, shift, axis):
    average = jnp.mean(values, axis=axis, keepdims=True)
    centred = values - average
    spread = jnp.mean(centred * centred, axis=axis, keepdims=True)
    return centred * lax.rsqrt(spread + EPSILON) * gain + shift


def low_lanes(shape):
    return lax.broadcasted_iota(jnp.int32, shape, len(shape) - 1) < HALF


def swap_halves(first, second):
    low, axis = low_lanes(first.shape), first.ndim - 1
    return (
        jnp.where(low, first, pltpu.roll(second, HALF, axis)),
        jnp.where(low, pltpu.roll(first, HALF, axis), second),
    )


def project(chunk, s, weight, gain, shift, weights, staged, normed_ref):
    normed = layer_norm(chunk, gain, shift, -1).astype(BF)
    normed_ref[s : s + 2] = normed.reshape(2, LANES, LANES)
    both = lax.dot_general(weights, normed, (((1,), (1,)), ((), ())), preferred_element_type=F32)
    halves = sigmoid(both[2 * LANES :]) * both[: 2 * LANES] * weight
    for n in range(2):
        part = halves[:, n * LANES : (n + 1) * LANES]
        staged[pl.ds(s + n, LANES, stride=2 * ROWS), :] = part[:LANES]
        staged[pl.ds(ROWS + s + n, LANES, stride=2 * ROWS), :] = part[LANES:]


def joined_weights(proj_in, gate_in):
    return jnp.concatenate([proj_in.T, gate_in.T], axis=0)


def pair_of(ref, s):
    return ref[s : s + 2].reshape(2 * LANES, LANES)


def residual(prior_ref, gates_ref, proj_out, wide, columns_ref, layer, s):
    parts = [wide[pl.ds(s + n, LANES, stride=ROWS), :] for n in range(2)]
    gain, shift = (jnp.concatenate([columns_ref[layer, n]] * 2, axis=1) for n in range(2))
    mixed = layer_norm(jnp.concatenate(parts, axis=1), gain, shift, 0).astype(BF)
    update = lax.dot_general(mixed, proj_out, (((0,), (0,)), ((), ())), preferred_element_type=F32)
    return pair_of(prior_ref, s) + pair_of(gates_ref, s) * update


def tokens_of(pair_ref, s):
    return jnp.concatenate(
        [pair_ref[pl.ds(b * ROWS + s, HALF, stride=2 * ROWS), :] for b in range(2)], axis=0
    )


def first_kernel(
    pair_hbm, mask_hbm, lanes_hbm, gain_hbm, shift_hbm, out_gain_hbm, out_shift_hbm, proj_hbm, gate_hbm,
    send_ref, normed_ref, weight_ref, vectors_ref,
    pair_ref, mask_vec, mask_smem, gain, shift, out_gain, out_shift, proj_in, gate_in, staged, arrived,
):
    moves = [
        (proj_hbm.at[0], proj_in),
        (gate_hbm.at[0], gate_in),
        (pair_hbm, pair_ref),
        (mask_hbm, mask_smem),
        (lanes_hbm, mask_vec),
        (gain_hbm, gain),
        (shift_hbm, shift),
        (out_gain_hbm, out_gain),
        (out_shift_hbm, out_shift),
    ]
    copies = [
        pltpu.make_async_copy(src, dst, arrived.at[n]) for n, (src, dst) in enumerate(moves)
    ]
    for copy in copies:
        copy.start()
    for copy in copies[:2]:
        copy.wait()
    weights = joined_weights(proj_in[...], gate_in[...])
    for copy in copies[2:]:
        copy.wait()
    row, core = lax.axis_index(("h", "x")), lax.axis_index("core")
    chip = lax.axis_index("z") * 2 + lax.axis_index("y")
    low = low_lanes((1, LANES))
    tokens = mask_vec[pl.ds(row // 2, 1), :].astype(F32)
    own = jnp.where(low == (row % 2 == 0), tokens, pltpu.roll(tokens, HALF, 1))
    begin = (chip * 2 + core) * (2 * ROWS)
    for s in range(0, ROWS, 2):
        both = []
        for n in range(2):
            first = mask_smem[begin + s + n].astype(F32)
            second = mask_smem[begin + ROWS + s + n].astype(F32)
            weight = own * jnp.where(low, first, second)
            weight_ref[pl.ds(s + n, 1), :] = weight
            both.append(weight)
        chunk = jnp.concatenate([tokens_of(pair_ref, s), tokens_of(pair_ref, s + 1)], axis=0)
        weight = jnp.concatenate(both, axis=1)
        project(chunk, s, weight, gain[0:1], shift[0:1], weights, staged, normed_ref)
    send_ref[...] = staged[...].astype(BF).reshape(send_ref.shape)
    for n, ref in enumerate((gain, shift, out_gain, out_shift)):
        vectors_ref[pl.ds(2 * n, 2), :] = ref[...]


def gates_of(normed_ref, gate_out, gates_ref):
    for s in range(0, ROWS, 2):
        gating = jnp.dot(pair_of(normed_ref, s), gate_out[0], preferred_element_type=F32)
        gates_ref[s : s + 2] = sigmoid(gating).reshape(2, LANES, LANES)


def second_kernel(
    back_ref, prior_ref, gates_ref, weights_ref, columns_ref, weight_ref, vectors_ref, proj_out,
    send_ref, normed_ref, pass_ref, staged, wide,
):
    wide[...] = back_ref[...].astype(F32).reshape(wide.shape)
    gain, shift = vectors_ref[pl.ds(1, 1), :], vectors_ref[pl.ds(3, 1), :]
    for s in range(0, ROWS, 2):
        first_pass = residual(prior_ref, gates_ref, proj_out[0], wide, columns_ref, 0, s)
        pass_ref[s : s + 2] = first_pass.reshape(2, LANES, LANES)
        weight = jnp.concatenate([weight_ref[pl.ds(s + n, 1), :] for n in range(2)], axis=1)
        project(first_pass, s, weight, gain, shift, weights_ref[...], staged, normed_ref)
    send_ref[...] = staged[...].astype(BF).reshape(send_ref.shape)


def third_kernel(back_ref, pass_ref, gates_ref, columns_ref, proj_out, out_ref, wide):
    wide[...] = back_ref[...].astype(F32).reshape(wide.shape)
    for s in range(0, ROWS, 2):
        updated = residual(pass_ref, gates_ref, proj_out[0], wide, columns_ref, 1, s)
        for n in range(4):
            place = n % 2 * ROWS + s + n // 2
            out_ref[pl.ds(place, HALF, stride=2 * ROWS), :] = updated[n * HALF : (n + 1) * HALF]


def of_row(row, wide_x):
    at = {"h": LISTS["h"].index(row // wide_x), "x": LISTS["x"].index(row % wide_x)}
    return tuple(at.get(axis, slice(None)) for axis in ORDER)


def columns_first(block):
    if ORDER.index("z") > ORDER.index("y"):
        block = jnp.swapaxes(block, 0, 1)
    zs, ys = ([LISTS[axis].index(n) for n in range(len(LISTS[axis]))] for axis in "zy")
    return jnp.stack([jnp.stack([block[z, y] for y in ys]) for z in zs])


def as_listed(block):
    block = jnp.stack([jnp.stack([block[z, y] for y in LISTS["y"]]) for z in LISTS["z"]])
    return jnp.swapaxes(block, 0, 1) if ORDER.index("z") > ORDER.index("y") else block


def gather_rows(ref, half, store):
    wide_x = ref.shape[ORDER.index("x")]
    rows = slice(half * ROWS, (half + 1) * ROWS)
    for m in range(ROWS // 2):
        first = columns_first(ref[of_row(2 * m, wide_x)].astype(F32))
        second = columns_first(ref[of_row(2 * m + 1, wide_x)].astype(F32))
        low, high = swap_halves(first[:, :, rows], second[:, :, rows])
        store(pl.ds(m * LANES, LANES), jnp.concatenate([low, high], axis=2).astype(BF))


def scatter_rows(product, out_ref):
    wide_x = out_ref.shape[ORDER.index("x")]
    for m in range(ROWS // 2):
        part = product[..., m * LANES : (m + 1) * LANES]
        even, odd = swap_halves(part[:, :, :ROWS], part[:, :, ROWS:])
        out_ref[of_row(2 * m, wide_x)] = as_listed(even.astype(BF))
        out_ref[of_row(2 * m + 1, wide_x)] = as_listed(odd.astype(BF))


def keep_in(ref):
    def store(lanes, tile):
        ref[:, :, :, lanes] = tile

    return store


def outgoing_share_kernel(own_ref, mine_ref, theirs_ref, left, right, total):
    gather_rows(own_ref, 0, keep_in(left))
    gather_rows(own_ref, 1, keep_in(right))
    tokens = left.shape[-1]
    lefts, rights = left[...].reshape(-1, tokens), right[...].reshape(-1, tokens)
    total[...] = lax.dot_general(
        rights, lefts, (((0,), (0,)), ((), ())), preferred_element_type=F32
    ).reshape(total.shape)
    core = lax.axis_index("core")
    theirs_ref[...] = total[:, :, 1 - core].astype(BF)
    mine_ref[...] = total[:, :, core]


def aside_kernel(
    pair_ref, normed_ref, gate_out, proj_in, gate_in, vectors_ref,
    prior_ref, gates_ref, weights_ref, columns_ref,
):
    gates_of(normed_ref, gate_out, gates_ref)
    for s in range(ROWS):
        prior_ref[s] = tokens_of(pair_ref, s)
    weights_ref[...] = joined_weights(proj_in[0], gate_in[0])
    for layer in range(2):
        for n in range(2):
            row_vec = vectors_ref[pl.ds(4 + 2 * n + layer, 1), :]
            columns_ref[layer, n] = jnp.broadcast_to(row_vec, (LANES, LANES)).T


def outgoing_kernel(mine_ref, other_ref, out_ref):
    scatter_rows(mine_ref[...] + other_ref[...].astype(F32), out_ref)


def incoming_left_kernel(own_ref, left_ref):
    gather_rows(own_ref, 0, keep_in(left_ref))


def incoming_right_kernel(own_ref, normed_ref, gate_out, right_ref, gates_ref):
    gather_rows(own_ref, 1, keep_in(right_ref))
    gates_of(normed_ref, gate_out, gates_ref)


def incoming_kernel(left_ref, other_ref, right_ref, out_ref, left):
    core = lax.axis_index("core")
    left[:, :, core] = left_ref[...]
    left[:, :, 1 - core] = other_ref[...]
    tokens = left.shape[-1]
    lefts, rights = left[...].reshape(-1, tokens), right_ref[...].reshape(-1, tokens)
    product = lax.dot_general(rights, lefts, (((1,), (1,)), ((), ())), preferred_element_type=F32)
    scatter_rows(product.reshape(right_ref.shape), out_ref)


def whole(shape):
    return pl.BlockSpec(shape, lambda i: (0,) * len(shape))


def layer_of(array, layer):
    return pl.BlockSpec((1, *array.shape[1:]), lambda i: (layer, 0, 0))


HBM = pl.BlockSpec(memory_space=pltpu.HBM)


def call(body, in_specs, out_shapes, scratch, name, flops=None):
    cost = None
    if flops is not None:
        cost = pl.CostEstimate(flops=flops, bytes_accessed=4 * 2**20, transcendentals=2**17)
    return pl.pallas_call(
        body,
        grid=(1,),
        in_specs=in_specs,
        out_specs=[whole(o.shape) for o in out_shapes],
        out_shape=out_shapes,
        scratch_shapes=scratch,
        compiler_params=pltpu.CompilerParams(vmem_limit_bytes=VMEM_LIMIT),
        cost_estimate=cost,
        name=name,
    )


def on_device(chips, pair_field, token_mask, gain, shift, proj_in, gate_in, out_gain, out_shift, gate_out, proj_out):
    tokens = pair_field.shape[0] * pair_field.shape[1]
    channels = pair_field.shape[2]
    pairs = pair_field.reshape(tokens, channels)
    mask_vec = token_mask.reshape(-1, LANES)
    axes = ("h", "x", "z", "y", "core")
    sizes = {axis: lax.axis_size(axis) for axis in axes}
    by_chip = tuple(sizes[axis] for axis in ORDER)
    places = np.arange(2 * chips).reshape([sizes[axis] for axis in axes])
    places = places[np.ix_(*(LISTS.get(axis, range(2)) for axis in axes))]
    places = places.transpose([axes.index(axis) for axis in (*ORDER, "core")])
    groups = places.reshape(chips, 2).T.tolist()
    n = token_mask.shape[0]
    own_columns = (sizes["z"], 2, 2 * ROWS, n)
    all_columns = (sizes["z"], 2, 2, 2 * ROWS, n)

    shape = jax.ShapeDtypeStruct
    send = shape((chips, 2 * ROWS, LANES), BF)
    sent_by_chip = shape(by_chip + send.shape[1:], BF)
    back = shape((chips, ROWS, LANES), BF)
    back_by_chip = shape(by_chip + back.shape[1:], BF)
    kept = shape((ROWS, LANES, channels), BF)
    kept_wide = shape(kept.shape, F32)
    joined = shape((4 * channels, channels), BF)
    columns = shape((2, 2, channels, LANES), F32)
    rows = shape((ROWS, LANES), F32)
    staged = pltpu.VMEM((channels * 2 * ROWS, LANES), F32)
    wide = pltpu.VMEM((channels * ROWS, LANES), F32)
    own_half = pltpu.VMEM(own_columns, BF)
    total = pltpu.VMEM(all_columns, F32)
    flops = 2 * tokens * channels * channels

    def exchange(x):
        return lax.all_to_all(x, axes, 0, 0, axis_index_groups=groups, tiled=True)

    def swap_cores(x):
        return lax.ppermute(x, "core", [(0, 1), (1, 0)])

    sent, normed, weights, vectors = call(
        first_kernel,
        [HBM] * 9,
        [send, kept, rows, rows],
        [
            pltpu.VMEM(pairs.shape, F32),
            pltpu.VMEM(mask_vec.shape, jnp.int32),
            pltpu.SMEM(token_mask.shape, jnp.int32),
            *[pltpu.VMEM(gain.shape, F32)] * 4,
            pltpu.VMEM(proj_in.shape[1:], BF),
            pltpu.VMEM(gate_in.shape[1:], BF),
            staged,
            pltpu.SemaphoreType.DMA((9,)),
        ],
        "project_first",
    )(*(
        pltpu.with_memory_space_constraint(x, pltpu.HBM)
        for x in (pairs, token_mask, mask_vec, gain, shift, out_gain, out_shift, proj_in, gate_in)
    ))

    mine, pairs, normed = lax.optimization_barrier((exchange(sent), pairs, normed))
    mine, theirs = call(
        outgoing_share_kernel,
        [whole(sent_by_chip.shape)],
        [shape(own_columns, F32), shape(own_columns, BF)],
        [own_half, own_half, total],
        "outgoing_share",
    )(mine.reshape(sent_by_chip.shape))
    mine, theirs, pairs, normed = lax.optimization_barrier((mine, theirs, pairs, normed))
    other = swap_cores(theirs)
    made = call(
        aside_kernel,
        [
            whole(pairs.shape), whole(kept.shape), layer_of(gate_out, 0),
            layer_of(proj_in, 1), layer_of(gate_in, 1), whole(rows.shape),
        ],
        [kept_wide, kept_wide, joined, columns],
        [],
        "aside",
        flops,
    )(pairs, normed, gate_out, proj_in, gate_in, vectors)
    other, (prior, gates, second_weights, column_vectors) = lax.optimization_barrier((other, made))
    (result,) = call(
        outgoing_kernel,
        [whole(own_columns)] * 2,
        [back_by_chip],
        [],
        "outgoing",
    )(mine, other)
    combined = exchange(result.reshape(back.shape))
    sent, normed, first_pass = call(
        second_kernel,
        [
            whole(back.shape), whole(kept.shape), whole(kept.shape), whole(joined.shape),
            whole(columns.shape), whole(rows.shape), whole(rows.shape), layer_of(proj_out, 0),
        ],
        [send, kept, kept_wide],
        [staged, wide],
        "finish_and_project",
    )(combined, prior, gates, second_weights, column_vectors, weights, vectors, proj_out)

    mine, normed = lax.optimization_barrier((exchange(sent).reshape(sent_by_chip.shape), normed))
    (left,) = call(
        incoming_left_kernel,
        [whole(sent_by_chip.shape)],
        [shape(own_columns, BF)],
        [],
        "incoming_left",
    )(mine)
    mine, left, normed = lax.optimization_barrier((mine, left, normed))
    other = swap_cores(left)
    made = call(
        incoming_right_kernel,
        [whole(sent_by_chip.shape), whole(kept.shape), layer_of(gate_out, 1)],
        [shape(own_columns, BF), kept_wide],
        [],
        "incoming_right",
        flops,
    )(mine, normed, gate_out)
    other, (right, gates) = lax.optimization_barrier((other, made))
    (result,) = call(
        incoming_kernel,
        [whole(own_columns)] * 3,
        [back_by_chip],
        [pltpu.VMEM(all_columns, BF)],
        "incoming",
    )(left, other, right)
    combined = exchange(result.reshape(back.shape))
    (updated,) = call(
        third_kernel,
        [whole(back.shape), whole(kept.shape), whole(kept.shape), whole(columns.shape), layer_of(proj_out, 1)],
        [shape(pairs.shape, F32)],
        [wide],
        "finish",
    )(combined, first_pass, gates, column_vectors, proj_out)
    return updated.reshape(pair_field.shape)


def solution(mesh):
    rows, cols = mesh.devices.shape
    devices = np.asarray(mesh.devices).reshape(2, rows // 2, cols // 4, 2, 2)
    spec = P(("h", "x"), ("z", "y", "core"), None)
    return jax.shard_map(
        functools.partial(on_device, rows * cols // 2),
        mesh=Mesh(devices, ("h", "x", "z", "y", "core")),
        in_specs=(spec,) + (P(),) * 9,
        out_specs=spec,
        check_vma=False,
    )
```

```python
import functools

import jax
import jax.numpy as jnp
import numpy as np
from jax import lax
from jax.experimental import pallas as pl
from jax.experimental.pallas import tpu as pltpu
from jax.sharding import Mesh
from jax.sharding import PartitionSpec as P

EPSILON = 1e-05
ROWS, LANES, HALF = 8, 128, 64
BF, F32 = jnp.bfloat16, jnp.float32
VMEM_LIMIT = 40 * 1024 * 1024
ORDER = ("z", "h", "x", "y")
LISTS = {"z": (5, 1, 6, 2, 7, 3, 0, 4), "y": (0, 1), "h": (1, 0), "x": (2, 3, 0, 1)}


def sigmoid(x):
    return 0.5 * jnp.tanh(0.5 * x) + 0.5


def layer_norm(values, gain, shift, axis):
    average = jnp.mean(values, axis=axis, keepdims=True)
    centred = values - average
    spread = jnp.mean(centred * centred, axis=axis, keepdims=True)
    return centred * lax.rsqrt(spread + EPSILON) * gain + shift


def low_lanes(shape):
    return lax.broadcasted_iota(jnp.int32, shape, len(shape) - 1) < HALF


def swap_halves(first, second):
    low, axis = low_lanes(first.shape), first.ndim - 1
    return (
        jnp.where(low, first, pltpu.roll(second, HALF, axis)),
        jnp.where(low, pltpu.roll(first, HALF, axis), second),
    )


def project(chunk, s, weight, gain, shift, weights, staged, normed_ref):
    normed = layer_norm(chunk, gain, shift, -1).astype(BF)
    normed_ref[s : s + 2] = normed.reshape(2, LANES, LANES)
    both = lax.dot_general(weights, normed, (((1,), (1,)), ((), ())), preferred_element_type=F32)
    halves = (jnp.tanh(both[2 * LANES :]) + 1.0) * (both[: 2 * LANES] * weight)
    for n in range(2):
        part = halves[:, n * LANES : (n + 1) * LANES]
        staged[pl.ds(s + n, LANES, stride=2 * ROWS), :] = part[:LANES]
        staged[pl.ds(ROWS + s + n, LANES, stride=2 * ROWS), :] = part[LANES:]


def joined_weights(proj_in, gate_in):
    return jnp.concatenate([proj_in.T, gate_in.T * jnp.bfloat16(0.5)], axis=0)


def pair_of(ref, s):
    return ref[s : s + 2].reshape(2 * LANES, LANES)


def residual(prior_ref, gates_ref, proj_out, wide, columns_ref, layer, s):
    parts = [wide[pl.ds(s + n, LANES, stride=ROWS), :] for n in range(2)]
    gain, shift = (jnp.concatenate([columns_ref[layer, n]] * 2, axis=1) for n in range(2))
    mixed = layer_norm(jnp.concatenate(parts, axis=1), gain, shift, 0).astype(BF)
    update = lax.dot_general(mixed, proj_out, (((0,), (0,)), ((), ())), preferred_element_type=F32)
    return pair_of(prior_ref, s) + pair_of(gates_ref, s) * update


def tokens_of(pair_ref, s):
    return jnp.concatenate(
        [pair_ref[pl.ds(b * ROWS + s, HALF, stride=2 * ROWS), :] for b in range(2)], axis=0
    )


def first_kernel(
    pair_hbm, mask_hbm, lanes_hbm, gain_hbm, shift_hbm, out_gain_hbm, out_shift_hbm, proj_hbm, gate_hbm,
    send_ref, normed_ref, weight_ref, vectors_ref,
    pair_ref, mask_vec, mask_smem, gain, shift, out_gain, out_shift, proj_in, gate_in, staged, arrived,
):
    moves = [
        (proj_hbm.at[0], proj_in),
        (gate_hbm.at[0], gate_in),
        (pair_hbm, pair_ref),
        (mask_hbm, mask_smem),
        (lanes_hbm, mask_vec),
        (gain_hbm, gain),
        (shift_hbm, shift),
        (out_gain_hbm, out_gain),
        (out_shift_hbm, out_shift),
    ]
    copies = [
        pltpu.make_async_copy(src, dst, arrived.at[n]) for n, (src, dst) in enumerate(moves)
    ]
    for copy in copies:
        copy.start()
    for copy in copies[:2]:
        copy.wait()
    weights = joined_weights(proj_in[...], gate_in[...])
    for copy in copies[2:]:
        copy.wait()
    row, core = lax.axis_index(("h", "x")), lax.axis_index("core")
    chip = lax.axis_index("z") * 2 + lax.axis_index("y")
    low = low_lanes((1, LANES))
    tokens = mask_vec[pl.ds(row // 2, 1), :].astype(F32)
    own = jnp.where(low == (row % 2 == 0), tokens, pltpu.roll(tokens, HALF, 1))
    begin = (chip * 2 + core) * (2 * ROWS)
    for s in range(0, ROWS, 2):
        both = []
        for n in range(2):
            first = mask_smem[begin + s + n].astype(F32)
            second = mask_smem[begin + ROWS + s + n].astype(F32)
            weight = own * jnp.where(low, 0.5 * first, 0.5 * second)
            weight_ref[pl.ds(s + n, 1), :] = weight
            both.append(weight)
        chunk = jnp.concatenate([tokens_of(pair_ref, s), tokens_of(pair_ref, s + 1)], axis=0)
        weight = jnp.concatenate(both, axis=1)
        project(chunk, s, weight, gain[0:1], shift[0:1], weights, staged, normed_ref)
    send_ref[...] = staged[...].astype(BF).reshape(send_ref.shape)
    for n, ref in enumerate((gain, shift, out_gain, out_shift)):
        vectors_ref[pl.ds(2 * n, 2), :] = ref[...]


def gates_of(normed_ref, gate_out, gates_ref):
    for s in range(0, ROWS, 2):
        gating = jnp.dot(pair_of(normed_ref, s), gate_out[0], preferred_element_type=F32)
        gates_ref[s : s + 2] = sigmoid(gating).reshape(2, LANES, LANES)


def second_kernel(
    back_ref, prior_ref, gates_ref, weights_ref, columns_ref, weight_ref, vectors_ref, proj_out,
    send_ref, normed_ref, pass_ref, staged, wide,
):
    wide[...] = back_ref[...].astype(F32).reshape(wide.shape)
    gain, shift = vectors_ref[pl.ds(1, 1), :], vectors_ref[pl.ds(3, 1), :]
    for s in range(0, ROWS, 2):
        first_pass = residual(prior_ref, gates_ref, proj_out[0], wide, columns_ref, 0, s)
        pass_ref[s : s + 2] = first_pass.reshape(2, LANES, LANES)
        weight = jnp.concatenate([weight_ref[pl.ds(s + n, 1), :] for n in range(2)], axis=1)
        project(first_pass, s, weight, gain, shift, weights_ref[...], staged, normed_ref)
    send_ref[...] = staged[...].astype(BF).reshape(send_ref.shape)


def third_kernel(back_ref, pass_ref, gates_ref, columns_ref, proj_out, out_ref, wide):
    wide[...] = back_ref[...].astype(F32).reshape(wide.shape)
    for s in range(0, ROWS, 2):
        updated = residual(pass_ref, gates_ref, proj_out[0], wide, columns_ref, 1, s)
        for n in range(4):
            place = n % 2 * ROWS + s + n // 2
            out_ref[pl.ds(place, HALF, stride=2 * ROWS), :] = updated[n * HALF : (n + 1) * HALF]


def of_row(row, wide_x):
    at = {"h": LISTS["h"].index(row // wide_x), "x": LISTS["x"].index(row % wide_x)}
    return tuple(at.get(axis, slice(None)) for axis in ORDER)


def columns_first(block):
    if ORDER.index("z") > ORDER.index("y"):
        block = jnp.swapaxes(block, 0, 1)
    zs, ys = ([LISTS[axis].index(n) for n in range(len(LISTS[axis]))] for axis in "zy")
    return jnp.stack([jnp.stack([block[z, y] for y in ys]) for z in zs])


def as_listed(block):
    block = jnp.stack([jnp.stack([block[z, y] for y in LISTS["y"]]) for z in LISTS["z"]])
    return jnp.swapaxes(block, 0, 1) if ORDER.index("z") > ORDER.index("y") else block


def gather_rows(ref, half, store):
    wide_x = ref.shape[ORDER.index("x")]
    rows = slice(half * ROWS, (half + 1) * ROWS)
    for m in range(ROWS // 2):
        first = columns_first(ref[of_row(2 * m, wide_x)].astype(F32))
        second = columns_first(ref[of_row(2 * m + 1, wide_x)].astype(F32))
        low, high = swap_halves(first[:, :, rows], second[:, :, rows])
        store(pl.ds(m * LANES, LANES), jnp.concatenate([low, high], axis=2).astype(BF))


def scatter_rows(product, out_ref):
    wide_x = out_ref.shape[ORDER.index("x")]
    for m in range(ROWS // 2):
        part = product[..., m * LANES : (m + 1) * LANES]
        even, odd = swap_halves(part[:, :, :ROWS], part[:, :, ROWS:])
        out_ref[of_row(2 * m, wide_x)] = as_listed(even.astype(BF))
        out_ref[of_row(2 * m + 1, wide_x)] = as_listed(odd.astype(BF))


def keep_in(ref):
    def store(lanes, tile):
        ref[:, :, :, lanes] = tile

    return store


def outgoing_share_kernel(own_ref, mine_ref, theirs_ref, left, right, total):
    gather_rows(own_ref, 0, keep_in(left))
    gather_rows(own_ref, 1, keep_in(right))
    tokens = left.shape[-1]
    lefts, rights = left[...].reshape(-1, tokens), right[...].reshape(-1, tokens)
    total[...] = lax.dot_general(
        rights, lefts, (((0,), (0,)), ((), ())), preferred_element_type=F32
    ).reshape(total.shape)
    core = lax.axis_index("core")
    theirs_ref[...] = total[:, :, 1 - core].astype(BF)
    mine_ref[...] = total[:, :, core]


def aside_kernel(
    pair_ref, normed_ref, gate_out, proj_in, gate_in, vectors_ref,
    prior_ref, gates_ref, weights_ref, columns_ref,
):
    gates_of(normed_ref, gate_out, gates_ref)
    for s in range(ROWS):
        prior_ref[s] = tokens_of(pair_ref, s)
    weights_ref[...] = joined_weights(proj_in[0], gate_in[0])
    for layer in range(2):
        for n in range(2):
            row_vec = vectors_ref[pl.ds(4 + 2 * n + layer, 1), :]
            columns_ref[layer, n] = jnp.broadcast_to(row_vec, (LANES, LANES)).T


def outgoing_kernel(mine_ref, other_ref, out_ref):
    scatter_rows(mine_ref[...] + other_ref[...].astype(F32), out_ref)


def incoming_left_kernel(own_ref, left_ref):
    gather_rows(own_ref, 0, keep_in(left_ref))


def incoming_right_kernel(own_ref, normed_ref, gate_out, right_ref, gates_ref):
    gather_rows(own_ref, 1, keep_in(right_ref))
    gates_of(normed_ref, gate_out, gates_ref)


def incoming_kernel(left_ref, other_ref, right_ref, out_ref, left):
    core = lax.axis_index("core")
    left[:, :, core] = left_ref[...]
    left[:, :, 1 - core] = other_ref[...]
    tokens = left.shape[-1]
    lefts, rights = left[...].reshape(-1, tokens), right_ref[...].reshape(-1, tokens)
    product = lax.dot_general(rights, lefts, (((1,), (1,)), ((), ())), preferred_element_type=F32)
    scatter_rows(product.reshape(right_ref.shape), out_ref)


def whole(shape):
    return pl.BlockSpec(shape, lambda i: (0,) * len(shape))


def layer_of(array, layer):
    return pl.BlockSpec((1, *array.shape[1:]), lambda i: (layer, 0, 0))


HBM = pl.BlockSpec(memory_space=pltpu.HBM)


def call(body, in_specs, out_shapes, scratch, name, flops=None):
    cost = None
    if flops is not None:
        cost = pl.CostEstimate(flops=flops, bytes_accessed=4 * 2**20, transcendentals=2**17)
    return pl.pallas_call(
        body,
        grid=(1,),
        in_specs=in_specs,
        out_specs=[whole(o.shape) for o in out_shapes],
        out_shape=out_shapes,
        scratch_shapes=scratch,
        compiler_params=pltpu.CompilerParams(vmem_limit_bytes=VMEM_LIMIT),
        cost_estimate=cost,
        name=name,
    )


def on_device(chips, pair_field, token_mask, gain, shift, proj_in, gate_in, out_gain, out_shift, gate_out, proj_out):
    tokens = pair_field.shape[0] * pair_field.shape[1]
    channels = pair_field.shape[2]
    pairs = pair_field.reshape(tokens, channels)
    mask_vec = token_mask.reshape(-1, LANES)
    axes = ("h", "x", "z", "y", "core")
    sizes = {axis: lax.axis_size(axis) for axis in axes}
    by_chip = tuple(sizes[axis] for axis in ORDER)
    places = np.arange(2 * chips).reshape([sizes[axis] for axis in axes])
    places = places[np.ix_(*(LISTS.get(axis, range(2)) for axis in axes))]
    places = places.transpose([axes.index(axis) for axis in (*ORDER, "core")])
    groups = places.reshape(chips, 2).T.tolist()
    n = token_mask.shape[0]
    own_columns = (sizes["z"], 2, 2 * ROWS, n)
    all_columns = (sizes["z"], 2, 2, 2 * ROWS, n)

    shape = jax.ShapeDtypeStruct
    send = shape((chips, 2 * ROWS, LANES), BF)
    sent_by_chip = shape(by_chip + send.shape[1:], BF)
    back = shape((chips, ROWS, LANES), BF)
    back_by_chip = shape(by_chip + back.shape[1:], BF)
    kept = shape((ROWS, LANES, channels), BF)
    kept_wide = shape(kept.shape, F32)
    joined = shape((4 * channels, channels), BF)
    columns = shape((2, 2, channels, LANES), F32)
    rows = shape((ROWS, LANES), F32)
    staged = pltpu.VMEM((channels * 2 * ROWS, LANES), F32)
    wide = pltpu.VMEM((channels * ROWS, LANES), F32)
    own_half = pltpu.VMEM(own_columns, BF)
    total = pltpu.VMEM(all_columns, F32)
    flops = 2 * tokens * channels * channels

    def exchange(x):
        return lax.all_to_all(x, axes, 0, 0, axis_index_groups=groups, tiled=True)

    def swap_cores(x):
        return lax.ppermute(x, "core", [(0, 1), (1, 0)])

    sent, normed, weights, vectors = call(
        first_kernel,
        [HBM] * 9,
        [send, kept, rows, rows],
        [
            pltpu.VMEM(pairs.shape, F32),
            pltpu.VMEM(mask_vec.shape, jnp.int32),
            pltpu.SMEM(token_mask.shape, jnp.int32),
            *[pltpu.VMEM(gain.shape, F32)] * 4,
            pltpu.VMEM(proj_in.shape[1:], BF),
            pltpu.VMEM(gate_in.shape[1:], BF),
            staged,
            pltpu.SemaphoreType.DMA((9,)),
        ],
        "project_first",
    )(*(
        pltpu.with_memory_space_constraint(x, pltpu.HBM)
        for x in (pairs, token_mask, mask_vec, gain, shift, out_gain, out_shift, proj_in, gate_in)
    ))

    mine, pairs, normed = lax.optimization_barrier((exchange(sent), pairs, normed))
    mine, theirs = call(
        outgoing_share_kernel,
        [whole(sent_by_chip.shape)],
        [shape(own_columns, F32), shape(own_columns, BF)],
        [own_half, own_half, total],
        "outgoing_share",
    )(mine.reshape(sent_by_chip.shape))
    mine, theirs, pairs, normed = lax.optimization_barrier((mine, theirs, pairs, normed))
    other = swap_cores(theirs)
    made = call(
        aside_kernel,
        [
            whole(pairs.shape), whole(kept.shape), layer_of(gate_out, 0),
            layer_of(proj_in, 1), layer_of(gate_in, 1), whole(rows.shape),
        ],
        [kept_wide, kept_wide, joined, columns],
        [],
        "aside",
        flops,
    )(pairs, normed, gate_out, proj_in, gate_in, vectors)
    other, (prior, gates, second_weights, column_vectors) = lax.optimization_barrier((other, made))
    (result,) = call(
        outgoing_kernel,
        [whole(own_columns)] * 2,
        [back_by_chip],
        [],
        "outgoing",
    )(mine, other)
    combined = exchange(result.reshape(back.shape))
    sent, normed, first_pass = call(
        second_kernel,
        [
            whole(back.shape), whole(kept.shape), whole(kept.shape), whole(joined.shape),
            whole(columns.shape), whole(rows.shape), whole(rows.shape), layer_of(proj_out, 0),
        ],
        [send, kept, kept_wide],
        [staged, wide],
        "finish_and_project",
    )(combined, prior, gates, second_weights, column_vectors, weights, vectors, proj_out)

    mine, normed = lax.optimization_barrier((exchange(sent).reshape(sent_by_chip.shape), normed))
    (left,) = call(
        incoming_left_kernel,
        [whole(sent_by_chip.shape)],
        [shape(own_columns, BF)],
        [],
        "incoming_left",
    )(mine)
    mine, left, normed = lax.optimization_barrier((mine, left, normed))
    other = swap_cores(left)
    made = call(
        incoming_right_kernel,
        [whole(sent_by_chip.shape), whole(kept.shape), layer_of(gate_out, 1)],
        [shape(own_columns, BF), kept_wide],
        [],
        "incoming_right",
        flops,
    )(mine, normed, gate_out)
    other, (right, gates) = lax.optimization_barrier((other, made))
    (result,) = call(
        incoming_kernel,
        [whole(own_columns)] * 3,
        [back_by_chip],
        [pltpu.VMEM(all_columns, BF)],
        "incoming",
    )(left, other, right)
    combined = exchange(result.reshape(back.shape))
    (updated,) = call(
        third_kernel,
        [whole(back.shape), whole(kept.shape), whole(kept.shape), whole(columns.shape), layer_of(proj_out, 1)],
        [shape(pairs.shape, F32)],
        [wide],
        "finish",
    )(combined, first_pass, gates, column_vectors, proj_out)
    return updated.reshape(pair_field.shape)


def solution(mesh):
    rows, cols = mesh.devices.shape
    devices = np.asarray(mesh.devices).reshape(2, rows // 2, cols // 4, 2, 2)
    spec = P(("h", "x"), ("z", "y", "core"), None)
    return jax.shard_map(
        functools.partial(on_device, rows * cols // 2),
        mesh=Mesh(devices, ("h", "x", "z", "y", "core")),
        in_specs=(spec,) + (P(),) * 9,
        out_specs=spec,
        check_vma=False,
    )
```

```python
import functools

import jax
import jax.numpy as jnp
import numpy as np
from jax import lax
from jax.experimental import pallas as pl
from jax.experimental.pallas import tpu as pltpu
from jax.sharding import Mesh
from jax.sharding import PartitionSpec as P

EPSILON = 1e-05
ROWS, LANES, HALF = 8, 128, 64
BF, F32 = jnp.bfloat16, jnp.float32
VMEM_LIMIT = 40 * 1024 * 1024
ORDER = ("z", "h", "x", "y")
LISTS = {"z": (5, 1, 4, 0, 3, 7, 2, 6), "y": (0, 1), "h": (1, 0), "x": (2, 3, 0, 1)}


def sigmoid(x):
    return 0.5 * jnp.tanh(0.5 * x) + 0.5


def layer_norm(values, gain, shift, axis):
    average = jnp.mean(values, axis=axis, keepdims=True)
    centred = values - average
    spread = jnp.mean(centred * centred, axis=axis, keepdims=True)
    return centred * lax.rsqrt(spread + EPSILON) * gain + shift


def low_lanes(shape):
    return lax.broadcasted_iota(jnp.int32, shape, len(shape) - 1) < HALF


def swap_halves(first, second):
    low, axis = low_lanes(first.shape), first.ndim - 1
    return (
        jnp.where(low, first, pltpu.roll(second, HALF, axis)),
        jnp.where(low, pltpu.roll(first, HALF, axis), second),
    )


def project(chunk, s, weight, gain, shift, weights, staged, normed_ref):
    normed = layer_norm(chunk, gain, shift, -1).astype(BF)
    normed_ref[s : s + 2] = normed.reshape(2, LANES, LANES)
    both = lax.dot_general(weights, normed, (((1,), (1,)), ((), ())), preferred_element_type=F32)
    halves = (jnp.tanh(both[2 * LANES :]) + 1.0) * (both[: 2 * LANES] * weight)
    for n in range(2):
        part = halves[:, n * LANES : (n + 1) * LANES]
        staged[pl.ds(s + n, LANES, stride=2 * ROWS), :] = part[:LANES]
        staged[pl.ds(ROWS + s + n, LANES, stride=2 * ROWS), :] = part[LANES:]


def joined_weights(proj_in, gate_in):
    return jnp.concatenate([proj_in.T, gate_in.T * jnp.bfloat16(0.5)], axis=0)


def pair_of(ref, s):
    return ref[s : s + 2].reshape(2 * LANES, LANES)


def residual(prior_ref, gates_ref, proj_out, wide, columns_ref, layer, s):
    parts = [wide[pl.ds(s + n, LANES, stride=ROWS), :] for n in range(2)]
    gain, shift = (jnp.concatenate([columns_ref[layer, n]] * 2, axis=1) for n in range(2))
    mixed = layer_norm(jnp.concatenate(parts, axis=1), gain, shift, 0).astype(BF)
    update = lax.dot_general(mixed, proj_out, (((0,), (0,)), ((), ())), preferred_element_type=F32)
    return pair_of(prior_ref, s) + pair_of(gates_ref, s) * update


def tokens_of(pair_ref, s):
    return jnp.concatenate(
        [pair_ref[pl.ds(b * ROWS + s, HALF, stride=2 * ROWS), :] for b in range(2)], axis=0
    )


def first_kernel(
    pair_hbm, mask_hbm, lanes_hbm, gain_hbm, shift_hbm, out_gain_hbm, out_shift_hbm, proj_hbm, gate_hbm,
    send_ref, normed_ref, weight_ref, vectors_ref,
    pair_ref, mask_vec, mask_smem, gain, shift, out_gain, out_shift, proj_in, gate_in, staged, arrived,
):
    moves = [
        (proj_hbm.at[0], proj_in),
        (gate_hbm.at[0], gate_in),
        (pair_hbm, pair_ref),
        (mask_hbm, mask_smem),
        (lanes_hbm, mask_vec),
        (gain_hbm, gain),
        (shift_hbm, shift),
        (out_gain_hbm, out_gain),
        (out_shift_hbm, out_shift),
    ]
    copies = [
        pltpu.make_async_copy(src, dst, arrived.at[n]) for n, (src, dst) in enumerate(moves)
    ]
    for copy in copies:
        copy.start()
    for copy in copies[:2]:
        copy.wait()
    weights = joined_weights(proj_in[...], gate_in[...])
    for copy in copies[2:]:
        copy.wait()
    row, core = lax.axis_index(("h", "x")), lax.axis_index("core")
    chip = lax.axis_index("z") * 2 + lax.axis_index("y")
    low = low_lanes((1, LANES))
    tokens = mask_vec[pl.ds(row // 2, 1), :].astype(F32)
    own = jnp.where(low == (row % 2 == 0), tokens, pltpu.roll(tokens, HALF, 1))
    begin = (chip * 2 + core) * (2 * ROWS)
    for s in range(0, ROWS, 2):
        both = []
        for n in range(2):
            first = mask_smem[begin + s + n].astype(F32)
            second = mask_smem[begin + ROWS + s + n].astype(F32)
            weight = own * jnp.where(low, 0.5 * first, 0.5 * second)
            weight_ref[pl.ds(s + n, 1), :] = weight
            both.append(weight)
        chunk = jnp.concatenate([tokens_of(pair_ref, s), tokens_of(pair_ref, s + 1)], axis=0)
        weight = jnp.concatenate(both, axis=1)
        project(chunk, s, weight, gain[0:1], shift[0:1], weights, staged, normed_ref)
    send_ref[...] = staged[...].astype(BF).reshape(send_ref.shape)
    for n, ref in enumerate((gain, shift, out_gain, out_shift)):
        vectors_ref[pl.ds(2 * n, 2), :] = ref[...]


def gates_of(normed_ref, gate_out, gates_ref):
    for s in range(0, ROWS, 2):
        gating = jnp.dot(pair_of(normed_ref, s), gate_out[0], preferred_element_type=F32)
        gates_ref[s : s + 2] = sigmoid(gating).reshape(2, LANES, LANES)


def second_kernel(
    back_ref, prior_ref, gates_ref, weights_ref, columns_ref, weight_ref, vectors_ref, proj_out,
    send_ref, normed_ref, pass_ref, staged, wide,
):
    wide[...] = back_ref[...].astype(F32).reshape(wide.shape)
    gain, shift = vectors_ref[pl.ds(1, 1), :], vectors_ref[pl.ds(3, 1), :]
    for s in range(0, ROWS, 2):
        first_pass = residual(prior_ref, gates_ref, proj_out[0], wide, columns_ref, 0, s)
        pass_ref[s : s + 2] = first_pass.reshape(2, LANES, LANES)
        weight = jnp.concatenate([weight_ref[pl.ds(s + n, 1), :] for n in range(2)], axis=1)
        project(first_pass, s, weight, gain, shift, weights_ref[...], staged, normed_ref)
    send_ref[...] = staged[...].astype(BF).reshape(send_ref.shape)


def third_kernel(back_ref, pass_ref, gates_ref, columns_ref, proj_out, out_ref, wide):
    wide[...] = back_ref[...].astype(F32).reshape(wide.shape)
    for s in range(0, ROWS, 2):
        updated = residual(pass_ref, gates_ref, proj_out[0], wide, columns_ref, 1, s)
        for n in range(4):
            place = n % 2 * ROWS + s + n // 2
            out_ref[pl.ds(place, HALF, stride=2 * ROWS), :] = updated[n * HALF : (n + 1) * HALF]


def of_row(row, wide_x):
    at = {"h": LISTS["h"].index(row // wide_x), "x": LISTS["x"].index(row % wide_x)}
    return tuple(at.get(axis, slice(None)) for axis in ORDER)


def columns_first(block):
    if ORDER.index("z") > ORDER.index("y"):
        block = jnp.swapaxes(block, 0, 1)
    zs, ys = ([LISTS[axis].index(n) for n in range(len(LISTS[axis]))] for axis in "zy")
    return jnp.stack([jnp.stack([block[z, y] for y in ys]) for z in zs])


def as_listed(block):
    block = jnp.stack([jnp.stack([block[z, y] for y in LISTS["y"]]) for z in LISTS["z"]])
    return jnp.swapaxes(block, 0, 1) if ORDER.index("z") > ORDER.index("y") else block


def gather_rows(ref, half, store):
    wide_x = ref.shape[ORDER.index("x")]
    rows = slice(half * ROWS, (half + 1) * ROWS)
    for m in range(ROWS // 2):
        first = columns_first(ref[of_row(2 * m, wide_x)].astype(F32))
        second = columns_first(ref[of_row(2 * m + 1, wide_x)].astype(F32))
        low, high = swap_halves(first[:, :, rows], second[:, :, rows])
        store(pl.ds(m * LANES, LANES), jnp.concatenate([low, high], axis=2).astype(BF))


def scatter_rows(product, out_ref):
    wide_x = out_ref.shape[ORDER.index("x")]
    for m in range(ROWS // 2):
        part = product[..., m * LANES : (m + 1) * LANES]
        even, odd = swap_halves(part[:, :, :ROWS], part[:, :, ROWS:])
        out_ref[of_row(2 * m, wide_x)] = as_listed(even.astype(BF))
        out_ref[of_row(2 * m + 1, wide_x)] = as_listed(odd.astype(BF))


def keep_in(ref):
    def store(lanes, tile):
        ref[:, :, :, lanes] = tile

    return store


def outgoing_share_kernel(own_ref, mine_ref, theirs_ref, left, right, total):
    gather_rows(own_ref, 0, keep_in(left))
    gather_rows(own_ref, 1, keep_in(right))
    tokens = left.shape[-1]
    lefts, rights = left[...].reshape(-1, tokens), right[...].reshape(-1, tokens)
    total[...] = lax.dot_general(
        rights, lefts, (((0,), (0,)), ((), ())), preferred_element_type=F32
    ).reshape(total.shape)
    core = lax.axis_index("core")
    theirs_ref[...] = total[:, :, 1 - core].astype(BF)
    mine_ref[...] = total[:, :, core]


def aside_kernel(
    pair_ref, normed_ref, gate_out, proj_in, gate_in, vectors_ref,
    prior_ref, gates_ref, weights_ref, columns_ref,
):
    gates_of(normed_ref, gate_out, gates_ref)
    for s in range(ROWS):
        prior_ref[s] = tokens_of(pair_ref, s)
    weights_ref[...] = joined_weights(proj_in[0], gate_in[0])
    for layer in range(2):
        for n in range(2):
            row_vec = vectors_ref[pl.ds(4 + 2 * n + layer, 1), :]
            columns_ref[layer, n] = jnp.broadcast_to(row_vec, (LANES, LANES)).T


def outgoing_kernel(mine_ref, other_ref, out_ref):
    scatter_rows(mine_ref[...] + other_ref[...].astype(F32), out_ref)


def incoming_left_kernel(own_ref, left_ref):
    gather_rows(own_ref, 0, keep_in(left_ref))


def incoming_right_kernel(own_ref, normed_ref, gate_out, right_ref, gates_ref):
    gather_rows(own_ref, 1, keep_in(right_ref))
    gates_of(normed_ref, gate_out, gates_ref)


def incoming_kernel(left_ref, other_ref, right_ref, out_ref, left):
    core = lax.axis_index("core")
    left[:, :, core] = left_ref[...]
    left[:, :, 1 - core] = other_ref[...]
    tokens = left.shape[-1]
    lefts, rights = left[...].reshape(-1, tokens), right_ref[...].reshape(-1, tokens)
    product = lax.dot_general(rights, lefts, (((1,), (1,)), ((), ())), preferred_element_type=F32)
    scatter_rows(product.reshape(right_ref.shape), out_ref)


def whole(shape):
    return pl.BlockSpec(shape, lambda i: (0,) * len(shape))


def layer_of(array, layer):
    return pl.BlockSpec((1, *array.shape[1:]), lambda i: (layer, 0, 0))


HBM = pl.BlockSpec(memory_space=pltpu.HBM)


def call(body, in_specs, out_shapes, scratch, name, flops=None):
    cost = None
    if flops is not None:
        cost = pl.CostEstimate(flops=flops, bytes_accessed=4 * 2**20, transcendentals=2**17)
    return pl.pallas_call(
        body,
        grid=(1,),
        in_specs=in_specs,
        out_specs=[whole(o.shape) for o in out_shapes],
        out_shape=out_shapes,
        scratch_shapes=scratch,
        compiler_params=pltpu.CompilerParams(vmem_limit_bytes=VMEM_LIMIT),
        cost_estimate=cost,
        name=name,
    )


def on_device(chips, pair_field, token_mask, gain, shift, proj_in, gate_in, out_gain, out_shift, gate_out, proj_out):
    tokens = pair_field.shape[0] * pair_field.shape[1]
    channels = pair_field.shape[2]
    pairs = pair_field.reshape(tokens, channels)
    mask_vec = token_mask.reshape(-1, LANES)
    axes = ("h", "x", "z", "y", "core")
    sizes = {axis: lax.axis_size(axis) for axis in axes}
    by_chip = tuple(sizes[axis] for axis in ORDER)
    places = np.arange(2 * chips).reshape([sizes[axis] for axis in axes])
    places = places[np.ix_(*(LISTS.get(axis, range(2)) for axis in axes))]
    places = places.transpose([axes.index(axis) for axis in (*ORDER, "core")])
    groups = places.reshape(chips, 2).T.tolist()
    n = token_mask.shape[0]
    own_columns = (sizes["z"], 2, 2 * ROWS, n)
    all_columns = (sizes["z"], 2, 2, 2 * ROWS, n)

    shape = jax.ShapeDtypeStruct
    send = shape((chips, 2 * ROWS, LANES), BF)
    sent_by_chip = shape(by_chip + send.shape[1:], BF)
    back = shape((chips, ROWS, LANES), BF)
    back_by_chip = shape(by_chip + back.shape[1:], BF)
    kept = shape((ROWS, LANES, channels), BF)
    kept_wide = shape(kept.shape, F32)
    joined = shape((4 * channels, channels), BF)
    columns = shape((2, 2, channels, LANES), F32)
    rows = shape((ROWS, LANES), F32)
    staged = pltpu.VMEM((channels * 2 * ROWS, LANES), F32)
    wide = pltpu.VMEM((channels * ROWS, LANES), F32)
    own_half = pltpu.VMEM(own_columns, BF)
    total = pltpu.VMEM(all_columns, F32)
    flops = 2 * tokens * channels * channels

    def exchange(x):
        return lax.all_to_all(x, axes, 0, 0, axis_index_groups=groups, tiled=True)

    def swap_cores(x):
        return lax.ppermute(x, "core", [(0, 1), (1, 0)])

    sent, normed, weights, vectors = call(
        first_kernel,
        [HBM] * 9,
        [send, kept, rows, rows],
        [
            pltpu.VMEM(pairs.shape, F32),
            pltpu.VMEM(mask_vec.shape, jnp.int32),
            pltpu.SMEM(token_mask.shape, jnp.int32),
            *[pltpu.VMEM(gain.shape, F32)] * 4,
            pltpu.VMEM(proj_in.shape[1:], BF),
            pltpu.VMEM(gate_in.shape[1:], BF),
            staged,
            pltpu.SemaphoreType.DMA((9,)),
        ],
        "project_first",
    )(*(
        pltpu.with_memory_space_constraint(x, pltpu.HBM)
        for x in (pairs, token_mask, mask_vec, gain, shift, out_gain, out_shift, proj_in, gate_in)
    ))

    mine, pairs, normed = lax.optimization_barrier((exchange(sent), pairs, normed))
    mine, theirs = call(
        outgoing_share_kernel,
        [whole(sent_by_chip.shape)],
        [shape(own_columns, F32), shape(own_columns, BF)],
        [own_half, own_half, total],
        "outgoing_share",
    )(mine.reshape(sent_by_chip.shape))
    mine, theirs, pairs, normed = lax.optimization_barrier((mine, theirs, pairs, normed))
    other = swap_cores(theirs)
    made = call(
        aside_kernel,
        [
            whole(pairs.shape), whole(kept.shape), layer_of(gate_out, 0),
            layer_of(proj_in, 1), layer_of(gate_in, 1), whole(rows.shape),
        ],
        [kept_wide, kept_wide, joined, columns],
        [],
        "aside",
        flops,
    )(pairs, normed, gate_out, proj_in, gate_in, vectors)
    other, (prior, gates, second_weights, column_vectors) = lax.optimization_barrier((other, made))
    (result,) = call(
        outgoing_kernel,
        [whole(own_columns)] * 2,
        [back_by_chip],
        [],
        "outgoing",
    )(mine, other)
    combined = exchange(result.reshape(back.shape))
    sent, normed, first_pass = call(
        second_kernel,
        [
            whole(back.shape), whole(kept.shape), whole(kept.shape), whole(joined.shape),
            whole(columns.shape), whole(rows.shape), whole(rows.shape), layer_of(proj_out, 0),
        ],
        [send, kept, kept_wide],
        [staged, wide],
        "finish_and_project",
    )(combined, prior, gates, second_weights, column_vectors, weights, vectors, proj_out)

    mine, normed = lax.optimization_barrier((exchange(sent).reshape(sent_by_chip.shape), normed))
    (left,) = call(
        incoming_left_kernel,
        [whole(sent_by_chip.shape)],
        [shape(own_columns, BF)],
        [],
        "incoming_left",
    )(mine)
    mine, left, normed = lax.optimization_barrier((mine, left, normed))
    other = swap_cores(left)
    made = call(
        incoming_right_kernel,
        [whole(sent_by_chip.shape), whole(kept.shape), layer_of(gate_out, 1)],
        [shape(own_columns, BF), kept_wide],
        [],
        "incoming_right",
        flops,
    )(mine, normed, gate_out)
    other, (right, gates) = lax.optimization_barrier((other, made))
    (result,) = call(
        incoming_kernel,
        [whole(own_columns)] * 3,
        [back_by_chip],
        [pltpu.VMEM(all_columns, BF)],
        "incoming",
    )(left, other, right)
    combined = exchange(result.reshape(back.shape))
    (updated,) = call(
        third_kernel,
        [whole(back.shape), whole(kept.shape), whole(kept.shape), whole(columns.shape), layer_of(proj_out, 1)],
        [shape(pairs.shape, F32)],
        [wide],
        "finish",
    )(combined, first_pass, gates, column_vectors, proj_out)
    return updated.reshape(pair_field.shape)


def solution(mesh):
    rows, cols = mesh.devices.shape
    devices = np.asarray(mesh.devices).reshape(2, rows // 2, cols // 4, 2, 2)
    spec = P(("h", "x"), ("z", "y", "core"), None)
    return jax.shard_map(
        functools.partial(on_device, rows * cols // 2),
        mesh=Mesh(devices, ("h", "x", "z", "y", "core")),
        in_specs=(spec,) + (P(),) * 9,
        out_specs=spec,
        check_vma=False,
    )
```

```python
import functools

import jax
import jax.numpy as jnp
import numpy as np
from jax import lax
from jax.experimental import pallas as pl
from jax.experimental.pallas import tpu as pltpu
from jax.sharding import Mesh
from jax.sharding import PartitionSpec as P

EPSILON = 1e-05
ROWS, LANES, HALF = 8, 128, 64
BF, F32 = jnp.bfloat16, jnp.float32
VMEM_LIMIT = 40 * 1024 * 1024
ORDER = ("z", "h", "x", "y")
LISTS = {"z": (5, 1, 6, 2, 7, 3, 0, 4), "y": (0, 1), "h": (1, 0), "x": (2, 3, 0, 1)}


def sigmoid(x):
    return 0.5 * jnp.tanh(0.5 * x) + 0.5


def layer_norm(values, gain, shift, axis):
    average = jnp.mean(values, axis=axis, keepdims=True)
    centred = values - average
    spread = jnp.mean(centred * centred, axis=axis, keepdims=True)
    return centred * lax.rsqrt(spread + EPSILON) * gain + shift


def low_lanes(shape):
    return lax.broadcasted_iota(jnp.int32, shape, len(shape) - 1) < HALF


def swap_halves(first, second):
    low, axis = low_lanes(first.shape), first.ndim - 1
    return (
        jnp.where(low, first, pltpu.roll(second, HALF, axis)),
        jnp.where(low, pltpu.roll(first, HALF, axis), second),
    )


def project(chunk, s, weight, gain, shift, weights, staged, normed_ref):
    normed = layer_norm(chunk, gain, shift, -1).astype(BF)
    normed_ref[s : s + 2] = normed.reshape(2, LANES, LANES)
    both = lax.dot_general(weights, normed, (((1,), (1,)), ((), ())), preferred_element_type=F32)
    halves = (jnp.tanh(both[2 * LANES :]) + 1.0) * (both[: 2 * LANES] * weight)
    for n in range(2):
        part = halves[:, n * LANES : (n + 1) * LANES]
        staged[pl.ds(s + n, LANES, stride=2 * ROWS), :] = part[:LANES]
        staged[pl.ds(ROWS + s + n, LANES, stride=2 * ROWS), :] = part[LANES:]


def joined_weights(proj_in, gate_in):
    return jnp.concatenate([proj_in.T, gate_in.T * jnp.bfloat16(0.5)], axis=0)


def pair_of(ref, s):
    return ref[s : s + 2].reshape(2 * LANES, LANES)


def residual(prior_ref, gates_ref, proj_out, wide, columns_ref, layer, s):
    parts = [wide[pl.ds(s + n, LANES, stride=ROWS), :] for n in range(2)]
    gain, shift = (jnp.concatenate([columns_ref[layer, n]] * 2, axis=1) for n in range(2))
    mixed = layer_norm(jnp.concatenate(parts, axis=1), gain, shift, 0).astype(BF)
    update = lax.dot_general(mixed, proj_out, (((0,), (0,)), ((), ())), preferred_element_type=F32)
    return pair_of(prior_ref, s) + pair_of(gates_ref, s) * update


def tokens_of(pair_ref, s):
    return jnp.concatenate(
        [pair_ref[pl.ds(b * ROWS + s, HALF, stride=2 * ROWS), :] for b in range(2)], axis=0
    )


def first_kernel(
    pair_hbm, mask_hbm, lanes_hbm, gain_hbm, shift_hbm, out_gain_hbm, out_shift_hbm, proj_hbm, gate_hbm,
    send_ref, normed_ref, weight_ref, vectors_ref,
    pair_ref, mask_vec, mask_smem, gain, shift, out_gain, out_shift, proj_in, gate_in, staged, arrived,
):
    moves = [
        (proj_hbm.at[0], proj_in),
        (gate_hbm.at[0], gate_in),
        (pair_hbm, pair_ref),
        (mask_hbm, mask_smem),
        (lanes_hbm, mask_vec),
        (gain_hbm, gain),
        (shift_hbm, shift),
        (out_gain_hbm, out_gain),
        (out_shift_hbm, out_shift),
    ]
    copies = [
        pltpu.make_async_copy(src, dst, arrived.at[n]) for n, (src, dst) in enumerate(moves)
    ]
    for copy in copies:
        copy.start()
    for copy in copies[:2]:
        copy.wait()
    weights = joined_weights(proj_in[...], gate_in[...])
    for copy in copies[2:7]:
        copy.wait()
    row, core = lax.axis_index(("h", "x")), lax.axis_index("core")
    chip = lax.axis_index("z") * 2 + lax.axis_index("y")
    low = low_lanes((1, LANES))
    tokens = mask_vec[pl.ds(row // 2, 1), :].astype(F32)
    own = jnp.where(low == (row % 2 == 0), tokens, pltpu.roll(tokens, HALF, 1))
    begin = (chip * 2 + core) * (2 * ROWS)
    for s in range(0, ROWS, 2):
        both = []
        for n in range(2):
            first = mask_smem[begin + s + n].astype(F32)
            second = mask_smem[begin + ROWS + s + n].astype(F32)
            weight = own * jnp.where(low, 0.5 * first, 0.5 * second)
            weight_ref[pl.ds(s + n, 1), :] = weight
            both.append(weight)
        chunk = jnp.concatenate([tokens_of(pair_ref, s), tokens_of(pair_ref, s + 1)], axis=0)
        weight = jnp.concatenate(both, axis=1)
        project(chunk, s, weight, gain[0:1], shift[0:1], weights, staged, normed_ref)
    send_ref[...] = staged[...].astype(BF).reshape(send_ref.shape)
    for copy in copies[7:]:
        copy.wait()
    for n, ref in enumerate((gain, shift, out_gain, out_shift)):
        vectors_ref[pl.ds(2 * n, 2), :] = ref[...]


def gates_of(normed_ref, gate_out, gates_ref):
    for s in range(0, ROWS, 2):
        gating = jnp.dot(pair_of(normed_ref, s), gate_out[0], preferred_element_type=F32)
        gates_ref[s : s + 2] = sigmoid(gating).reshape(2, LANES, LANES)


def second_kernel(
    back_ref, prior_ref, gates_ref, weights_ref, columns_ref, weight_ref, vectors_ref, proj_out,
    send_ref, normed_ref, pass_ref, staged, wide,
):
    wide[...] = back_ref[...].astype(F32).reshape(wide.shape)
    gain, shift = vectors_ref[pl.ds(1, 1), :], vectors_ref[pl.ds(3, 1), :]
    for s in range(0, ROWS, 2):
        first_pass = residual(prior_ref, gates_ref, proj_out[0], wide, columns_ref, 0, s)
        pass_ref[s : s + 2] = first_pass.reshape(2, LANES, LANES)
        weight = jnp.concatenate([weight_ref[pl.ds(s + n, 1), :] for n in range(2)], axis=1)
        project(first_pass, s, weight, gain, shift, weights_ref[...], staged, normed_ref)
    send_ref[...] = staged[...].astype(BF).reshape(send_ref.shape)


def third_kernel(back_ref, pass_ref, gates_ref, columns_ref, proj_out, out_ref, wide):
    wide[...] = back_ref[...].astype(F32).reshape(wide.shape)
    for s in range(0, ROWS, 2):
        updated = residual(pass_ref, gates_ref, proj_out[0], wide, columns_ref, 1, s)
        for n in range(4):
            place = n % 2 * ROWS + s + n // 2
            out_ref[pl.ds(place, HALF, stride=2 * ROWS), :] = updated[n * HALF : (n + 1) * HALF]


def of_row(row, wide_x):
    at = {"h": LISTS["h"].index(row // wide_x), "x": LISTS["x"].index(row % wide_x)}
    return tuple(at.get(axis, slice(None)) for axis in ORDER)


def columns_first(block):
    if ORDER.index("z") > ORDER.index("y"):
        block = jnp.swapaxes(block, 0, 1)
    zs, ys = ([LISTS[axis].index(n) for n in range(len(LISTS[axis]))] for axis in "zy")
    return jnp.stack([jnp.stack([block[z, y] for y in ys]) for z in zs])


def as_listed(block):
    block = jnp.stack([jnp.stack([block[z, y] for y in LISTS["y"]]) for z in LISTS["z"]])
    return jnp.swapaxes(block, 0, 1) if ORDER.index("z") > ORDER.index("y") else block


def gather_rows(ref, half, store):
    wide_x = ref.shape[ORDER.index("x")]
    rows = slice(half * ROWS, (half + 1) * ROWS)
    for m in range(ROWS // 2):
        first = columns_first(ref[of_row(2 * m, wide_x)].astype(F32))
        second = columns_first(ref[of_row(2 * m + 1, wide_x)].astype(F32))
        low, high = swap_halves(first[:, :, rows], second[:, :, rows])
        store(pl.ds(m * LANES, LANES), jnp.concatenate([low, high], axis=2).astype(BF))


def scatter_rows(product, out_ref):
    wide_x = out_ref.shape[ORDER.index("x")]
    for m in range(ROWS // 2):
        part = product[..., m * LANES : (m + 1) * LANES]
        even, odd = swap_halves(part[:, :, :ROWS], part[:, :, ROWS:])
        out_ref[of_row(2 * m, wide_x)] = as_listed(even.astype(BF))
        out_ref[of_row(2 * m + 1, wide_x)] = as_listed(odd.astype(BF))


def keep_in(ref):
    def store(lanes, tile):
        ref[:, :, :, lanes] = tile

    return store


def outgoing_share_kernel(own_ref, mine_ref, theirs_ref, left, right, total):
    gather_rows(own_ref, 0, keep_in(left))
    gather_rows(own_ref, 1, keep_in(right))
    tokens = left.shape[-1]
    lefts, rights = left[...].reshape(-1, tokens), right[...].reshape(-1, tokens)
    total[...] = lax.dot_general(
        rights, lefts, (((0,), (0,)), ((), ())), preferred_element_type=F32
    ).reshape(total.shape)
    core = lax.axis_index("core")
    theirs_ref[...] = total[:, :, 1 - core].astype(BF)
    mine_ref[...] = total[:, :, core]


def aside_kernel(
    pair_ref, normed_ref, gate_out, proj_in, gate_in, vectors_ref,
    prior_ref, gates_ref, weights_ref, columns_ref,
):
    gates_of(normed_ref, gate_out, gates_ref)
    for s in range(ROWS):
        prior_ref[s] = tokens_of(pair_ref, s)
    weights_ref[...] = joined_weights(proj_in[0], gate_in[0])
    for layer in range(2):
        for n in range(2):
            row_vec = vectors_ref[pl.ds(4 + 2 * n + layer, 1), :]
            columns_ref[layer, n] = jnp.broadcast_to(row_vec, (LANES, LANES)).T


def outgoing_kernel(mine_ref, other_ref, out_ref):
    scatter_rows(mine_ref[...] + other_ref[...].astype(F32), out_ref)


def incoming_left_kernel(own_ref, left_ref):
    gather_rows(own_ref, 0, keep_in(left_ref))


def incoming_right_kernel(own_ref, normed_ref, gate_out, right_ref, gates_ref):
    gather_rows(own_ref, 1, keep_in(right_ref))
    gates_of(normed_ref, gate_out, gates_ref)


def incoming_kernel(left_ref, other_ref, right_ref, out_ref, left):
    core = lax.axis_index("core")
    left[:, :, core] = left_ref[...]
    left[:, :, 1 - core] = other_ref[...]
    tokens = left.shape[-1]
    lefts, rights = left[...].reshape(-1, tokens), right_ref[...].reshape(-1, tokens)
    product = lax.dot_general(rights, lefts, (((1,), (1,)), ((), ())), preferred_element_type=F32)
    scatter_rows(product.reshape(right_ref.shape), out_ref)


def whole(shape):
    return pl.BlockSpec(shape, lambda i: (0,) * len(shape))


def layer_of(array, layer):
    return pl.BlockSpec((1, *array.shape[1:]), lambda i: (layer, 0, 0))


HBM = pl.BlockSpec(memory_space=pltpu.HBM)


def call(body, in_specs, out_shapes, scratch, name, flops=None):
    cost = None
    if flops is not None:
        cost = pl.CostEstimate(flops=flops, bytes_accessed=4 * 2**20, transcendentals=2**17)
    return pl.pallas_call(
        body,
        grid=(1,),
        in_specs=in_specs,
        out_specs=[whole(o.shape) for o in out_shapes],
        out_shape=out_shapes,
        scratch_shapes=scratch,
        compiler_params=pltpu.CompilerParams(vmem_limit_bytes=VMEM_LIMIT),
        cost_estimate=cost,
        name=name,
    )


def on_device(chips, pair_field, token_mask, gain, shift, proj_in, gate_in, out_gain, out_shift, gate_out, proj_out):
    tokens = pair_field.shape[0] * pair_field.shape[1]
    channels = pair_field.shape[2]
    pairs = pair_field.reshape(tokens, channels)
    mask_vec = token_mask.reshape(-1, LANES)
    axes = ("h", "x", "z", "y", "core")
    sizes = {axis: lax.axis_size(axis) for axis in axes}
    by_chip = tuple(sizes[axis] for axis in ORDER)
    places = np.arange(2 * chips).reshape([sizes[axis] for axis in axes])
    places = places[np.ix_(*(LISTS.get(axis, range(2)) for axis in axes))]
    places = places.transpose([axes.index(axis) for axis in (*ORDER, "core")])
    groups = places.reshape(chips, 2).T.tolist()
    n = token_mask.shape[0]
    own_columns = (sizes["z"], 2, 2 * ROWS, n)
    all_columns = (sizes["z"], 2, 2, 2 * ROWS, n)

    shape = jax.ShapeDtypeStruct
    send = shape((chips, 2 * ROWS, LANES), BF)
    sent_by_chip = shape(by_chip + send.shape[1:], BF)
    back = shape((chips, ROWS, LANES), BF)
    back_by_chip = shape(by_chip + back.shape[1:], BF)
    kept = shape((ROWS, LANES, channels), BF)
    kept_wide = shape(kept.shape, F32)
    joined = shape((4 * channels, channels), BF)
    columns = shape((2, 2, channels, LANES), F32)
    rows = shape((ROWS, LANES), F32)
    staged = pltpu.VMEM((channels * 2 * ROWS, LANES), F32)
    wide = pltpu.VMEM((channels * ROWS, LANES), F32)
    own_half = pltpu.VMEM(own_columns, BF)
    total = pltpu.VMEM(all_columns, F32)
    flops = 2 * tokens * channels * channels

    def exchange(x):
        return lax.all_to_all(x, axes, 0, 0, axis_index_groups=groups, tiled=True)

    def swap_cores(x):
        return lax.ppermute(x, "core", [(0, 1), (1, 0)])

    sent, normed, weights, vectors = call(
        first_kernel,
        [HBM] * 9,
        [send, kept, rows, rows],
        [
            pltpu.VMEM(pairs.shape, F32),
            pltpu.VMEM(mask_vec.shape, jnp.int32),
            pltpu.SMEM(token_mask.shape, jnp.int32),
            *[pltpu.VMEM(gain.shape, F32)] * 4,
            pltpu.VMEM(proj_in.shape[1:], BF),
            pltpu.VMEM(gate_in.shape[1:], BF),
            staged,
            pltpu.SemaphoreType.DMA((9,)),
        ],
        "project_first",
    )(*(
        pltpu.with_memory_space_constraint(x, pltpu.HBM)
        for x in (pairs, token_mask, mask_vec, gain, shift, out_gain, out_shift, proj_in, gate_in)
    ))

    mine, pairs, normed = lax.optimization_barrier((exchange(sent), pairs, normed))
    mine, theirs = call(
        outgoing_share_kernel,
        [whole(sent_by_chip.shape)],
        [shape(own_columns, F32), shape(own_columns, BF)],
        [own_half, own_half, total],
        "outgoing_share",
    )(mine.reshape(sent_by_chip.shape))
    mine, theirs, pairs, normed = lax.optimization_barrier((mine, theirs, pairs, normed))
    other = swap_cores(theirs)
    made = call(
        aside_kernel,
        [
            whole(pairs.shape), whole(kept.shape), layer_of(gate_out, 0),
            layer_of(proj_in, 1), layer_of(gate_in, 1), whole(rows.shape),
        ],
        [kept_wide, kept_wide, joined, columns],
        [],
        "aside",
        flops,
    )(pairs, normed, gate_out, proj_in, gate_in, vectors)
    other, (prior, gates, second_weights, column_vectors) = lax.optimization_barrier((other, made))
    (result,) = call(
        outgoing_kernel,
        [whole(own_columns)] * 2,
        [back_by_chip],
        [],
        "outgoing",
    )(mine, other)
    combined = exchange(result.reshape(back.shape))
    sent, normed, first_pass = call(
        second_kernel,
        [
            whole(back.shape), whole(kept.shape), whole(kept.shape), whole(joined.shape),
            whole(columns.shape), whole(rows.shape), whole(rows.shape), layer_of(proj_out, 0),
        ],
        [send, kept, kept_wide],
        [staged, wide],
        "finish_and_project",
    )(combined, prior, gates, second_weights, column_vectors, weights, vectors, proj_out)

    mine, normed = lax.optimization_barrier((exchange(sent).reshape(sent_by_chip.shape), normed))
    (left,) = call(
        incoming_left_kernel,
        [whole(sent_by_chip.shape)],
        [shape(own_columns, BF)],
        [],
        "incoming_left",
    )(mine)
    mine, left, normed = lax.optimization_barrier((mine, left, normed))
    other = swap_cores(left)
    made = call(
        incoming_right_kernel,
        [whole(sent_by_chip.shape), whole(kept.shape), layer_of(gate_out, 1)],
        [shape(own_columns, BF), kept_wide],
        [],
        "incoming_right",
        flops,
    )(mine, normed, gate_out)
    other, (right, gates) = lax.optimization_barrier((other, made))
    (result,) = call(
        incoming_kernel,
        [whole(own_columns)] * 3,
        [back_by_chip],
        [pltpu.VMEM(all_columns, BF)],
        "incoming",
    )(left, other, right)
    combined = exchange(result.reshape(back.shape))
    (updated,) = call(
        third_kernel,
        [whole(back.shape), whole(kept.shape), whole(kept.shape), whole(columns.shape), layer_of(proj_out, 1)],
        [shape(pairs.shape, F32)],
        [wide],
        "finish",
    )(combined, first_pass, gates, column_vectors, proj_out)
    return updated.reshape(pair_field.shape)


def solution(mesh):
    rows, cols = mesh.devices.shape
    devices = np.asarray(mesh.devices).reshape(2, rows // 2, cols // 4, 2, 2)
    spec = P(("h", "x"), ("z", "y", "core"), None)
    return jax.shard_map(
        functools.partial(on_device, rows * cols // 2),
        mesh=Mesh(devices, ("h", "x", "z", "y", "core")),
        in_specs=(spec,) + (P(),) * 9,
        out_specs=spec,
        check_vma=False,
    )
```
